256 devices in a mesh: ctx: 32 (over z, y_hi, core), ch: 8 (over x, y_lo).
Axes of the slice: x: 4, y: 4 (y_hi: 2, y_lo: 2; y = y_hi * 2 + y_lo), z: 8, core: 2. Of those that a mesh axis runs over, the one named last changes fastest.
Arguments:
- query_proj: bfloat16 [4096, 8192], P('ctx', 'ch'), may hold values from -6 to 6
- key_proj: bfloat16 [4096, 8192], P('ctx', 'ch'), may hold values from -6 to 6
- value_proj: bfloat16 [4096, 8192], P('ctx', 'ch'), may hold values from -6 to 6
- pole_rate: float32 [16, 8192], P(None, 'ch'), may hold values from 1.4648438e-06 to 0.05
- residue: float32 [16, 8192], P(None, 'ch'), may hold values from -2 to 2
- direct_gain: float32 [8192], P('ch'), may hold values from -4 to 4
- out_weight: bfloat16 [8192, 8192], P('ch', 'ctx'), may hold values from -0.125 to 0.125
Outputs:
- layer_out: bfloat16 [4096, 8192], P('ctx', 'ch')
The draws below stay inside these ranges and needn't reach their ends.
All inputs are finite; a program needn't handle non-finite values.
Results may differ from the reference program's by a relative error of at most 0.017.
Values may be sent and summed in bfloat16 or wider, within the bound.
A program may use at most 64 MiB of HBM per device.

```python
import math
import jax
import jax.numpy as jnp
from jax import lax

D = 8192
N_POLE = 16
SEQ = 4096
N_CH = 8


def with_spikes(entries, rng, source, target, shards_of, factor):
    owner, partner = [(jnp.arange(entries.shape[axis_at]) // (entries.shape[axis_at] // shards_of)).reshape([-1 if axis == axis_at else 1 for axis in range(entries.ndim)]) for axis_at in (source, target)]
    chosen = jax.random.permutation(rng, shards_of)[partner]
    strong = (owner == chosen) | (owner == (partner + shards_of // 2) % shards_of)
    return jnp.where(strong, factor * entries, entries)


def level_of(stream_key, shape, split, low, high):
    loudness = 1.0
    for position, parts in split:
        steps = jax.random.uniform(jax.random.fold_in(jax.random.fold_in(stream_key, 6), position), (parts,), jnp.float32, low / len(split), high / len(split))
        loudness = loudness * jnp.repeat(jnp.exp(steps), shape[position] // parts).reshape((-1,) + (1,) * (len(shape) - 1 - position))
    return loudness


def gaussian(stream_key, shape, spread, bound, shards=(), held_as=jnp.bfloat16):
    loudness = level_of(stream_key, shape, shards, -0.22, 0.18) if shards else 1.0
    entries = jax.random.normal(stream_key, shape, jnp.float32) * spread * loudness
    return jnp.minimum(jnp.maximum(entries, -bound), bound).astype(held_as)


def gaussian_with(stream_key, extent, scale, bound, pieces, heavy, kind=jnp.bfloat16):
    array = scale * jax.random.normal(stream_key, extent, jnp.float32)
    if pieces:
        array = array * level_of(stream_key, extent, pieces, -0.22, 0.18)
    return jnp.clip(with_spikes(array, jax.random.fold_in(stream_key, 3), *heavy), -bound, bound).astype(kind)


def setup_inputs(seed: int = 0) -> dict:
    streams_of = jax.random.split(jax.random.key(seed), 8)
    return {
        "query_proj": gaussian(streams_of[0], (SEQ, D), 1.0, 6.0, ((0, 32), (1, 8))),
        "key_proj": gaussian(streams_of[1], (SEQ, D), 1.0, 6.0, ((0, 32), (1, 8))),
        "value_proj": gaussian(streams_of[2], (SEQ, D), 1.0, 6.0, ((0, 32), (1, 8))),
        "pole_rate": jnp.clip(jnp.exp(math.log(0.05) - 10.4380297 * jax.random.uniform(streams_of[3], (N_POLE, D), jnp.float32) ** level_of(streams_of[3], (N_POLE, D), ((1, 8),), -0.2, 0.2)), 1.4648437627329258e-06, 0.05),
        "residue": gaussian(streams_of[4], (N_POLE, D), 0.3, 2.0, ((1, 8),), jnp.float32),
        "direct_gain": gaussian(streams_of[5], (D,), 1.0, 4.0, ((0, 8),), jnp.float32),
        "out_weight": gaussian_with(streams_of[6], (D, D), D ** -0.5, 0.125, ((0, 8), (1, 32)), (0, 1, 32, 2.75)),
    }


def link_pairs(earlier, later):
    return (earlier[0] * later[0], later[0] * earlier[1] + later[1])

def local_terms(stream, rate, coef, direct):
    block_len = 16
    length, width = stream.shape
    count = length // block_len
    grid = stream.reshape(count, block_len, width)
    steps = jnp.arange(block_len, dtype=jnp.float32)
    lag_decay = jnp.exp(-rate[:, None, :] * steps[None, :, None])
    taps = lax.optimization_barrier(jnp.sum(coef[:, None, :] * lag_decay, axis=0))
    inner = direct[None, None, :] * grid
    for lag in range(block_len):
        moved = jnp.pad(grid, ((0, 0), (lag, 0), (0, 0)))[:, :block_len]
        inner = inner + taps[lag][None, None, :] * moved
    weigh_in = jnp.exp(-rate[:, None, :] * (block_len - 1.0 - steps)[None, :, None])
    summary = jnp.zeros((rate.shape[0], count, width), jnp.float32)
    for place in range(block_len):
        summary = summary + weigh_in[:, place][:, None, :] * grid[:, place][None, :, :]
    step_decay = jnp.broadcast_to(jnp.exp(-rate * block_len)[:, None, :], summary.shape)
    _, ending = lax.associative_scan(link_pairs, (step_decay, summary), axis=1)
    before = jnp.concatenate([jnp.zeros_like(ending[:, :1]), ending[:, :-1]], axis=1)
    return (inner, before, ending[:, -1])

def add_entry(inner, before, rate, coef, entry):
    count, block_len, width = inner.shape
    steps = jnp.arange(block_len, dtype=jnp.float32)
    starts = jnp.arange(count, dtype=jnp.float32) * block_len
    before = before + jnp.exp(-rate[:, None, :] * starts[None, :, None]) * entry[:, None, :]
    weigh_out = coef[:, None, :] * jnp.exp(-rate[:, None, :] * (steps + 1.0)[None, :, None])
    outer = jnp.zeros((count, block_len, width), jnp.float32)
    for pole in range(rate.shape[0]):
        outer = outer + weigh_out[pole][None, :, :] * before[pole][:, None, :]
    return (inner + outer).reshape(count * block_len, width)

def reference(query_proj, key_proj, value_proj, pole_rate, residue, direct_gain, out_weight):
    coef = residue * jnp.sqrt(-jnp.expm1(-2.0 * pole_rate))
    group = D // N_CH

    def one_group(total, index):
        first = (index * group).astype(jnp.int32)
        query = lax.dynamic_slice_in_dim(query_proj, first, group, 1)
        keys = lax.dynamic_slice_in_dim(key_proj, first, group, 1)
        values = lax.dynamic_slice_in_dim(value_proj, first, group, 1)
        rate_g = lax.dynamic_slice_in_dim(pole_rate, first, group, 1)
        coef_g = lax.dynamic_slice_in_dim(coef, first, group, 1)
        direct_g = lax.dynamic_slice_in_dim(direct_gain, first, group, 0)
        weight_g = lax.dynamic_slice_in_dim(out_weight, first, group, 0)
        stream = keys.astype(jnp.float32) * values.astype(jnp.float32)
        inner, before, final = local_terms(stream, rate_g, coef_g, direct_g)
        conv = add_entry(inner, before, rate_g, coef_g, jnp.zeros_like(final))
        hidden = (query.astype(jnp.float32) * conv).astype(jnp.bfloat16)
        partial_g = jnp.dot(hidden, weight_g, preferred_element_type=jnp.float32).astype(jnp.bfloat16)
        partial_g = lax.optimization_barrier(partial_g)
        return (total + partial_g.astype(jnp.float32), None)
    start_total = jnp.zeros((SEQ, D), jnp.float32)
    total, _ = lax.scan(one_group, start_total, jnp.arange(N_CH, dtype=jnp.int32))
    return total.astype(jnp.bfloat16)
```

```python
import jax
import jax.numpy as jnp
from jax import lax
from jax.experimental import pallas as pl
from jax.experimental.pallas import tpu as pltpu
from jax.sharding import PartitionSpec as P

MESH = pl.DeviceIdType.MESH
BF = jnp.bfloat16
F32 = jnp.float32
POLES = 16
ROWS = 128
WIDTH = 1024
CHUNKS = 8
STEPS = 16
CTX = 32
OFFSETS = (0, -1, 1, -2, 2, -3, 3, 4)
ROUNDS = ((0,), (1, 2), (3, 4), (5, 6), (7,))


def one_minus_exp(x):
    series = 1.0 - x / 8.0
    for k in (7.0, 6.0, 5.0, 4.0, 3.0, 2.0):
        series = 1.0 - x / k * series
    return jnp.where(x < 0.125, x * series, 1.0 - jnp.exp(-x))


def spread(rows):
    return jnp.broadcast_to(rows[:, None, :], (POLES, CHUNKS, 128))


def kernel(
    q_hbm, k_hbm, v_hbm, rate_hbm, res_hbm, gain_hbm, w_hbm, out_hbm,
    qb, kb, vb, rate, res, gain, u, y, qf, before, lead,
    owned, fsend, frecv, esend, erecv, wbuf, abuf, pbuf,
    r1, r2, r3, p2, p3, p4,
    in_sem, w_send, w_recv, f_send, f_recv, e_send, e_recv,
    a_send, a_recv, x_send, x_recv, o_send, o_recv,
):
    ctx = lax.axis_index("ctx")
    ch = lax.axis_index("ch")
    z = lax.div(ctx, 4)
    q = lax.rem(ctx, 4)
    core = lax.rem(q, 2)
    y_hi = lax.div(q, 2)
    x = lax.div(ch, 2)
    y_lo = lax.rem(ch, 2)
    x0 = lax.rem(x, 2)
    x1 = lax.div(x, 2)
    near = lax.rem(x0 + x1, 2)
    far = x1
    near_ch = ch + 2 - 4 * x0
    far_ch = (3 - x) * 2 + y_lo
    y_ch = ch + 1 - 2 * y_lo
    sibling = ctx + 1 - 2 * core
    across = ctx + 2 - 4 * y_hi
    up = lax.rem(ctx + 4, CTX)
    down = lax.rem(ctx + CTX - 4, CTX)

    def block_at(j):
        return lax.rem(z + OFFSETS[j] + 8, 8)

    loads = []
    for place, (src, dst) in enumerate(
        ((k_hbm, kb), (v_hbm, vb), (rate_hbm, rate), (res_hbm, res), (gain_hbm, gain), (q_hbm, qb))
    ):
        loads.append(pltpu.make_async_copy(src, dst, in_sem.at[place]))
        loads[-1].start()
    w_own = pltpu.make_async_copy(w_hbm, wbuf.at[q], in_sem.at[6])
    w_own.start()

    bar = pltpu.get_barrier_semaphore()

    def greet(c, h):
        pl.semaphore_signal(bar, inc=1, device_id=(c, h), device_id_type=MESH)

    def greet_ctx(k, carry):
        greet(lax.rem(ctx + k, CTX), ch)
        return carry

    lax.fori_loop(1, CTX, greet_ctx, 0)
    for h in (near_ch, far_ch, y_ch):
        greet(ctx, h)
    is_home = ch == z

    def greet_ends(i, carry):
        @pl.when(jnp.logical_not(jnp.logical_and(is_home, i == z)))
        def _():
            greet(i * 4 + q, z)
            greet(ch * 4 + q, i)

        return carry

    lax.fori_loop(0, 8, greet_ends, 0)
    pl.semaphore_wait(bar, jnp.where(is_home, 34 + 14, 34 + 16))

    def w_copy(src, slot, place, target):
        return pltpu.make_async_remote_copy(
            src_ref=src, dst_ref=wbuf.at[slot], send_sem=w_send.at[place], recv_sem=w_recv.at[place],
            device_id=(target, ch), device_id_type=MESH,
        )

    w_across = w_copy(w_hbm, q, 0, across)
    w_across.start()
    w_sibling = w_copy(w_hbm, q, 1, sibling)
    w_sibling.start()

    for place in (0, 1, 2):
        loads[place].wait()
    chunk = lax.broadcasted_iota(jnp.int32, (POLES, CHUNKS, 128), 1)

    def lanes_of(g):
        return pl.ds(pl.multiple_of(g * 128, 128), 128)

    def tokens_at(p):
        return pl.ds(p, CHUNKS, stride=STEPS)

    def ending(g, carry):
        lanes = lanes_of(g)
        u[g] = kb[:, lanes].astype(F32) * vb[:, lanes].astype(F32)
        rows = rate[:, lanes]
        decay = spread(jnp.exp(-rows))
        state = jnp.zeros((POLES, CHUNKS, 128), F32)
        for p in range(STEPS):
            state = state * decay + u[g, tokens_at(p), :][None]
        for reach in (1, 2, 4):
            over = spread(jnp.exp(-rows * (STEPS * reach)))
            moved = pltpu.roll(state, reach, 1)
            state = state + jnp.where(chunk >= reach, over * moved, 0.0)
        before[g] = jnp.where(chunk >= 1, pltpu.roll(state, 1, 1), 0.0)
        owned[pl.ds(lax.div(g, 4) * POLES, POLES), lax.rem(g, 4), :] = rows
        fsend[pl.ds(lax.div(g, 4) * POLES, POLES), lax.rem(g, 4), :] = state[:, CHUNKS - 1, :]
        return carry

    lax.fori_loop(0, 8, ending, 0)

    def f_copy(k):
        owner = lax.rem(ctx + k, CTX)
        return pltpu.make_async_remote_copy(
            src_ref=fsend.at[owner], dst_ref=frecv.at[ctx], send_sem=f_send, recv_sem=f_recv,
            device_id=(owner, ch), device_id_type=MESH,
        )

    def f_start(k, carry):
        f_copy(k).start()
        return carry

    lax.fori_loop(1, CTX, f_start, 0)
    frecv[ctx] = fsend[ctx]

    for place in (3, 4, 5):
        loads[place].wait()

    def inside(g, carry):
        lanes = lanes_of(g)
        rows = rate[:, lanes]
        coef_rows = res[:, lanes] * jnp.sqrt(one_minus_exp(2.0 * rows))
        decay = spread(jnp.exp(-rows))
        coef = spread(coef_rows)
        lead[g] = coef * jnp.exp(-spread(rows) * (1.0 + STEPS * chunk.astype(F32)))
        direct = jnp.broadcast_to(gain[0:1, lanes], (CHUNKS, 128))
        qf[g] = qb[:, lanes].astype(F32)
        state = before[g]
        for p in range(STEPS):
            token = u[g, tokens_at(p), :]
            state = state * decay + token[None]
            y[g, tokens_at(p), :] = direct * token + jnp.sum(coef * state, axis=0)
        return carry

    lax.fori_loop(0, 4, inside, 0)

    bulk = pl.ds(0, CTX - 1)
    pltpu.make_async_copy(frecv.at[bulk], frecv.at[bulk], f_recv).wait()
    pltpu.make_async_copy(fsend.at[bulk], fsend.at[bulk], f_send).wait()
    own_decay = jnp.exp(-owned[ctx] * ROWS)
    entry = jnp.zeros((4, 128), F32)
    for i in range(CTX):
        esend[i] = entry
        entry = entry * own_decay + frecv[i]

    def e_start(k, carry):
        target = lax.rem(ctx + k, CTX)
        pltpu.make_async_remote_copy(
            src_ref=esend.at[target], dst_ref=erecv.at[ctx], send_sem=e_send, recv_sem=e_recv,
            device_id=(target, ch), device_id_type=MESH,
        ).start()
        return carry

    lax.fori_loop(1, CTX, e_start, 0)
    erecv[ctx] = esend[ctx]
    lax.fori_loop(4, 8, inside, 0)

    w_across.wait_recv()
    across_slot = lax.rem(q + 2, 4)
    w_onward = w_copy(wbuf.at[across_slot], across_slot, 2, sibling)
    w_onward.start()

    pltpu.make_async_copy(erecv.at[bulk], erecv.at[bulk], e_recv).wait()
    pltpu.make_async_copy(esend.at[bulk], esend.at[bulk], e_send).wait()

    def a_copy(r, way, c):
        src = 0 if r == 1 else 2 * (r - 1) - 1 + way
        dst = 7 if r == 4 else 2 * r - 1 + way
        place = ((r - 1) * 2 + way) * 2 + c
        return pltpu.make_async_remote_copy(
            src_ref=abuf.at[src, c], dst_ref=abuf.at[dst, c],
            send_sem=a_send.at[place], recv_sem=a_recv.at[place],
            device_id=((up, down)[way], ch), device_id_type=MESH,
        )

    def finish(c):
        def one(g, carry):
            lanes = lanes_of(g)
            decay = spread(jnp.exp(-rate[:, lanes]))
            rest = lead[g] * spread(erecv[pl.ds(lax.div(g, 4) * POLES, POLES), lax.rem(g, 4), :])
            for p in range(STEPS):
                y[g, tokens_at(p), :] = qf[g, tokens_at(p), :] * (
                    y[g, tokens_at(p), :] + jnp.sum(rest, axis=0)
                )
                rest = rest * decay
            abuf[0, c, :, lanes_of(lax.rem(g, 4))] = y[g].astype(BF)
            return carry

        lax.fori_loop(4 * c, 4 * c + 4, one, 0)

    a_copies = {}

    def a_go(r, way, c):
        a_copies[r, way, c] = a_copy(r, way, c)
        a_copies[r, way, c].start()

    for c in range(2):
        finish(c)
        for way in range(2):
            a_go(1, way, c)

    def a_arrive(r, c):
        for way in range(2):
            if r < 4 or way == c:
                a_copies[r, way, c].wait_recv()
                if r < 3 or (r == 3 and way == c):
                    a_go(r + 1, way, c)

    def product(slots):
        count = len(slots)

        def one(s, carry):
            for h in range(2):
                total = None
                for c in range(2):
                    left = jnp.concatenate([abuf[j, c] for j in slots], axis=0) if count > 1 else abuf[slots[0], c]
                    term = jnp.dot(
                        left, wbuf[2 * s + h, c * 512 : (c + 1) * 512, :], preferred_element_type=F32
                    )
                    total = term if total is None else total + term
                total = total.astype(BF)
                for n, j in enumerate(slots):
                    pbuf[j, s, :, h * 256 : (h + 1) * 256] = total[n * ROWS : (n + 1) * ROWS]
            return carry

        lax.fori_loop(0, 2, one, 0)

    first_bit = (near, far)
    second_bit = (far, near)
    first_ch = (near_ch, far_ch)
    second_ch = (far_ch, near_ch)

    def rows_at(bit, size):
        return pl.ds(pl.multiple_of(bit * size, size), size)

    x_copies = {}

    def x_go(stage, j, s):
        if stage == 1:
            src, dst, target = pbuf.at[j, s, rows_at(1 - first_bit[s], 64)], r1.at[j, s], first_ch[s]
        elif stage == 2:
            src, dst, target = p2.at[j, s, rows_at(1 - second_bit[s], 32)], r2.at[j, s], second_ch[s]
        else:
            src, dst, target = p3.at[j, s, rows_at(1 - y_lo, 16)], r3.at[j, s], y_ch
        place = ((stage - 1) * 8 + j) * 2 + s
        x_copies[stage, j, s] = pltpu.make_async_remote_copy(
            src_ref=src, dst_ref=dst, send_sem=x_send.at[place], recv_sem=x_recv.at[place],
            device_id=(ctx, target), device_id_type=MESH,
        )
        x_copies[stage, j, s].start()

    def x_take(stage, j, s):
        x_copies[stage, j, s].wait_recv()
        if stage == 1:
            mine, came, dst = pbuf[j, s, rows_at(first_bit[s], 64), :], r1[j, s], p2
        elif stage == 2:
            mine, came, dst = p2[j, s, rows_at(second_bit[s], 32), :], r2[j, s], p3
        else:
            mine, came, dst = p3[j, s, rows_at(y_lo, 16), :], r3[j, s], p4
        dst[j, s] = (mine.astype(F32) + came.astype(F32)).astype(BF)

    def step(stage, slots):
        for j in slots:
            for s in range(2):
                if stage:
                    x_take(stage, j, s)
                if stage < 3:
                    x_go(stage + 1, j, s)
                else:
                    place_out(j, s)

    def out_copy(j, s, local):
        rows = first_bit[s] * 64 + second_bit[s] * 32 + y_lo * 16
        dst = out_hbm.at[pl.ds(pl.multiple_of(rows, 16), 16), pl.ds(s * 512, 512)]
        if local:
            return pltpu.make_async_copy(p4.at[j, s], dst, o_recv)
        return pltpu.make_async_remote_copy(
            src_ref=p4.at[j, s], dst_ref=dst, send_sem=o_send, recv_sem=o_recv,
            device_id=(block_at(j) * 4 + q, z), device_id_type=MESH,
        )

    def place_out(j, s):
        if j:
            out_copy(j, s, False).start()
        else:
            @pl.when(is_home)
            def _():
                out_copy(j, s, True).start()

            @pl.when(jnp.logical_not(is_home))
            def _():
                out_copy(j, s, False).start()

    w_own.wait()
    w_sibling.wait_recv()
    w_onward.wait_recv()
    product(ROUNDS[0])
    step(0, ROUNDS[0])
    for r in (1, 2, 3, 4):
        a_arrive(r, 0)
        step(1, ROUNDS[r - 1])
        a_arrive(r, 1)
        product(ROUNDS[r])
        step(0, ROUNDS[r])
        step(2, ROUNDS[r - 1])
        if r >= 2:
            step(3, ROUNDS[r - 2])
    step(1, ROUNDS[4])
    step(3, ROUNDS[3])
    step(2, ROUNDS[4])
    step(3, ROUNDS[4])

    w_across.wait_send()
    w_sibling.wait_send()
    w_onward.wait_send()
    for copy in a_copies.values():
        copy.wait_send()
    for copy in x_copies.values():
        copy.wait_send()
    for j in range(8):
        for s in range(2):
            if j:
                out_copy(j, s, False).wait_send()
            else:
                @pl.when(jnp.logical_not(is_home))
                def _():
                    out_copy(j, s, False).wait_send()
    pltpu.make_async_copy(out_hbm, out_hbm, o_recv).wait()


def shards(query_proj, key_proj, value_proj, pole_rate, residue, direct_gain, out_weight):
    vmem = pltpu.VMEM
    dma = pltpu.SemaphoreType.DMA
    block = (ROWS, WIDTH)
    grouped = (8, ROWS, 128)
    tables = (8, POLES, CHUNKS, 128)
    return pl.pallas_call(
        kernel,
        out_shape=jax.ShapeDtypeStruct(block, BF),
        in_specs=[pl.BlockSpec(memory_space=pl.ANY)] * 7,
        out_specs=pl.BlockSpec(memory_space=pl.ANY),
        scratch_shapes=[
            vmem(block, BF), vmem(block, BF), vmem(block, BF),
            vmem((POLES, WIDTH), F32), vmem((POLES, WIDTH), F32), vmem((1, WIDTH), F32),
            vmem(grouped, F32), vmem(grouped, F32), vmem(grouped, F32),
            vmem(tables, F32), vmem(tables, F32),
            vmem((CTX, 4, 128), F32),
            vmem((CTX, 4, 128), F32), vmem((CTX, 4, 128), F32),
            vmem((CTX, 4, 128), F32), vmem((CTX, 4, 128), F32),
            vmem((4, WIDTH, 256), BF), vmem((8, 2, ROWS, 512), BF), vmem((8, 2, ROWS, 512), BF),
            vmem((8, 2, 64, 512), BF), vmem((8, 2, 32, 512), BF), vmem((8, 2, 16, 512), BF),
            vmem((8, 2, 64, 512), BF), vmem((8, 2, 32, 512), BF), vmem((8, 2, 16, 512), BF),
            dma((7,)), dma((3,)), dma((3,)), dma, dma, dma, dma,
            dma((16,)), dma((16,)), dma((48,)), dma((48,)), dma, dma,
        ],
        compiler_params=pltpu.CompilerParams(
            collective_id=0, has_side_effects=True, vmem_limit_bytes=40 * 1024 * 1024
        ),
        cost_estimate=pl.CostEstimate(flops=2**31, bytes_accessed=2**21, transcendentals=2**18),
    )(
        query_proj, key_proj, value_proj, pole_rate, residue,
        direct_gain.reshape(1, WIDTH), out_weight,
    )


def solution(mesh):
    return jax.shard_map(
        shards,
        mesh=mesh,
        in_specs=(
            P("ctx", "ch"),
            P("ctx", "ch"),
            P("ctx", "ch"),
            P(None, "ch"),
            P(None, "ch"),
            P("ch"),
            P("ch", "ctx"),
        ),
        out_specs=P("ctx", "ch"),
        check_vma=False,
    )
```

```python
import jax
import jax.numpy as jnp
from jax import lax
from jax.experimental import pallas as pl
from jax.experimental.pallas import tpu as pltpu
from jax.sharding import PartitionSpec as P

MESH = pl.DeviceIdType.MESH
BF = jnp.bfloat16
F32 = jnp.float32
POLES = 16
ROWS = 128
WIDTH = 1024
CHUNKS = 8
STEPS = 16
CTX = 32
PARTS = 4
AROUND = ((2, 1), (2, 0), (1, 1), (3, 1), (1, 0), (3, 0), (0, 1))
OFFSETS = (0, -1, 1, -2, 2, -3, 3, 4)
ROUNDS = ((0,), (1, 2), (3, 4), (5, 6), (7,))


def one_minus_exp(x):
    series = 1.0 - x / 8.0
    for k in (7.0, 6.0, 5.0, 4.0, 3.0, 2.0):
        series = 1.0 - x / k * series
    return jnp.where(x < 0.125, x * series, 1.0 - jnp.exp(-x))


def spread(rows):
    return jnp.broadcast_to(rows[:, None, :], (POLES, CHUNKS, 128))


def kernel(
    q_hbm, k_hbm, v_hbm, rate_hbm, res_hbm, gain_hbm, w_hbm, out_hbm,
    qb, kb, vb, rate, res, gain, u, y, qf, before, lead,
    owned, fsend, frecv, esend, erecv, wbuf, abuf, pbuf,
    rbuf, sums,
    in_sem, w_send, w_recv, f_send, f_recv, e_send, e_recv,
    a_send, a_recv, x_send, x_recv, o_send, o_recv,
):
    ctx = lax.axis_index("ctx")
    ch = lax.axis_index("ch")
    z = lax.div(ctx, 4)
    q = lax.rem(ctx, 4)
    core = lax.rem(q, 2)
    y_hi = lax.div(q, 2)
    x = lax.div(ch, 2)
    y_lo = lax.rem(ch, 2)
    sibling = ctx + 1 - 2 * core
    across = ctx + 2 - 4 * y_hi
    up = lax.rem(ctx + 4, CTX)
    down = lax.rem(ctx + CTX - 4, CTX)

    def block_at(j):
        return lax.rem(z + OFFSETS[j] + 8, 8)

    loads = []
    for place, (src, dst) in enumerate(
        ((k_hbm, kb), (v_hbm, vb), (rate_hbm, rate), (res_hbm, res), (gain_hbm, gain), (q_hbm, qb))
    ):
        loads.append(pltpu.make_async_copy(src, dst, in_sem.at[place]))
        loads[-1].start()
    w_own = pltpu.make_async_copy(w_hbm, wbuf.at[q], in_sem.at[6])
    w_own.start()

    bar = pltpu.get_barrier_semaphore()

    def greet(c, h):
        pl.semaphore_signal(bar, inc=1, device_id=(c, h), device_id_type=MESH)

    def greet_ctx(k, carry):
        greet(lax.rem(ctx + k, CTX), ch)
        return carry

    lax.fori_loop(1, CTX, greet_ctx, 0)
    def greet_ch(k, carry):
        greet(ctx, lax.rem(ch + k, 8))
        return carry

    lax.fori_loop(1, 8, greet_ch, 0)
    is_home = ch == z

    def greet_ends(i, carry):
        @pl.when(jnp.logical_not(jnp.logical_and(is_home, i == z)))
        def _():
            greet(i * 4 + q, z)
            greet(ch * 4 + q, i)

        return carry

    lax.fori_loop(0, 8, greet_ends, 0)
    pl.semaphore_wait(bar, jnp.where(is_home, 38 + 14, 38 + 16))

    for place in (0, 1, 2):
        loads[place].wait()
    chunk = lax.broadcasted_iota(jnp.int32, (POLES, CHUNKS, 128), 1)

    def lanes_of(g):
        return pl.ds(pl.multiple_of(g * 128, 128), 128)

    def tokens_at(p):
        return pl.ds(p, CHUNKS, stride=STEPS)

    def ending(g, carry):
        lanes = lanes_of(g)
        u[g] = kb[:, lanes].astype(F32) * vb[:, lanes].astype(F32)
        rows = rate[:, lanes]
        decay = spread(jnp.exp(-rows))
        state = jnp.zeros((POLES, CHUNKS, 128), F32)
        for p in range(STEPS):
            state = state * decay + u[g, tokens_at(p), :][None]
        for reach in (1, 2, 4):
            over = spread(jnp.exp(-rows * (STEPS * reach)))
            moved = pltpu.roll(state, reach, 1)
            state = state + jnp.where(chunk >= reach, over * moved, 0.0)
        before[g] = jnp.where(chunk >= 1, pltpu.roll(state, 1, 1), 0.0)
        owned[pl.ds(lax.div(g, 4) * POLES, POLES), lax.rem(g, 4), :] = rows
        fsend[pl.ds(lax.div(g, 4) * POLES, POLES), lax.rem(g, 4), :] = state[:, CHUNKS - 1, :]
        return carry

    lax.fori_loop(0, 8, ending, 0)

    def peer(k):
        t = lax.div(lax.rem(k, 16), 2)
        dz = 4 + lax.div(t + 1, 2) * (1 - 2 * lax.rem(t, 2))
        dy = 1 - lax.div(k, 16)
        dc = 1 - lax.rem(k, 2)
        return lax.rem(z + dz, 8) * 4 + lax.rem(y_hi + dy, 2) * 2 + lax.rem(core + dc, 2)

    def f_start(k, carry):
        owner = peer(k)
        pltpu.make_async_remote_copy(
            src_ref=fsend.at[owner], dst_ref=frecv.at[ctx], send_sem=f_send, recv_sem=f_recv,
            device_id=(owner, ch), device_id_type=MESH,
        ).start()
        return carry

    lax.fori_loop(0, CTX - 1, f_start, 0)

    def w_copy(src, slot, part, place, target):
        rows = pl.ds(part * 512, 512)
        return pltpu.make_async_remote_copy(
            src_ref=src.at[rows], dst_ref=wbuf.at[slot, rows],
            send_sem=w_send.at[place, part], recv_sem=w_recv.at[place, part],
            device_id=(target, ch), device_id_type=MESH,
        )

    w_across = [w_copy(w_hbm, q, part, 0, across) for part in range(2)]
    w_sibling = [w_copy(w_hbm, q, part, 1, sibling) for part in range(2)]
    w_across[0].start()
    frecv[ctx] = fsend[ctx]

    for place in (3, 4, 5):
        loads[place].wait()

    def inside(g, carry):
        lanes = lanes_of(g)
        rows = rate[:, lanes]
        coef_rows = res[:, lanes] * jnp.sqrt(one_minus_exp(2.0 * rows))
        decay = spread(jnp.exp(-rows))
        coef = spread(coef_rows)
        lead[g] = coef * jnp.exp(-spread(rows) * (1.0 + STEPS * chunk.astype(F32)))
        direct = jnp.broadcast_to(gain[0:1, lanes], (CHUNKS, 128))
        qf[g] = qb[:, lanes].astype(F32)
        state = before[g]
        for p in range(STEPS):
            token = u[g, tokens_at(p), :]
            state = state * decay + token[None]
            y[g, tokens_at(p), :] = direct * token + jnp.sum(coef * state, axis=0)
        return carry

    lax.fori_loop(0, 4, inside, 0)

    bulk = pl.ds(0, CTX - 1)
    pltpu.make_async_copy(frecv.at[bulk], frecv.at[bulk], f_recv).wait()
    pltpu.make_async_copy(fsend.at[bulk], fsend.at[bulk], f_send).wait()
    own_decay = jnp.exp(-owned[ctx] * ROWS)
    entry = jnp.zeros((4, 128), F32)
    for i in range(CTX):
        esend[i] = entry
        entry = entry * own_decay + frecv[i]

    def e_start(k, carry):
        target = peer(k)
        pltpu.make_async_remote_copy(
            src_ref=esend.at[target], dst_ref=erecv.at[ctx], send_sem=e_send, recv_sem=e_recv,
            device_id=(target, ch), device_id_type=MESH,
        ).start()
        return carry

    lax.fori_loop(0, CTX - 1, e_start, 0)
    w_across[1].start()
    for copy in w_sibling:
        copy.start()
    erecv[ctx] = esend[ctx]
    lax.fori_loop(4, 8, inside, 0)

    across_slot = lax.rem(q + 2, 4)
    w_onward = [w_copy(wbuf.at[across_slot], across_slot, part, 2, sibling) for part in range(2)]
    w_across[0].wait_recv()
    w_onward[0].start()

    pltpu.make_async_copy(erecv.at[bulk], erecv.at[bulk], e_recv).wait()
    pltpu.make_async_copy(esend.at[bulk], esend.at[bulk], e_send).wait()

    def a_copy(r, way, c):
        src = 0 if r == 1 else 2 * (r - 1) - 1 + way
        dst = 7 if r == 4 else 2 * r - 1 + way
        place = ((r - 1) * 2 + way) * PARTS + c
        return pltpu.make_async_remote_copy(
            src_ref=abuf.at[src, c], dst_ref=abuf.at[dst, c],
            send_sem=a_send.at[place], recv_sem=a_recv.at[place],
            device_id=((up, down)[way], ch), device_id_type=MESH,
        )

    def last_way(c):
        return c // (PARTS // 2)

    def finish(g, carry):
        lanes = lanes_of(g)
        decay = spread(jnp.exp(-rate[:, lanes]))
        rest = lead[g] * spread(erecv[pl.ds(lax.div(g, 4) * POLES, POLES), lax.rem(g, 4), :])
        for p in range(STEPS):
            y[g, tokens_at(p), :] = qf[g, tokens_at(p), :] * (
                y[g, tokens_at(p), :] + jnp.sum(rest, axis=0)
            )
            rest = rest * decay
        abuf[0, lax.div(g, 2), :, lanes_of(lax.rem(g, 2))] = y[g].astype(BF)
        return carry

    a_copies = {}

    def a_go(r, way, c):
        a_copies[r, way, c] = a_copy(r, way, c)
        a_copies[r, way, c].start()

    for c in range(PARTS):
        lax.fori_loop(2 * c, 2 * c + 2, finish, 0)
        for way in range(2):
            a_go(1, way, c)

    def a_arrive(r):
        for c in range(PARTS):
            for way in range(2):
                if r < 4 or way == last_way(c):
                    a_copies[r, way, c].wait_recv()
                    if r < 3 or (r == 3 and way == last_way(c)):
                        a_go(r + 1, way, c)

    def product(slots):
        def one(n, carry):
            total = None
            for c in range(PARTS):
                left = jnp.concatenate([abuf[j, c] for j in slots], axis=0) if len(slots) > 1 else abuf[slots[0], c]
                term = jnp.dot(
                    left, wbuf[n, c * 256 : (c + 1) * 256, :], preferred_element_type=F32
                )
                total = term if total is None else total + term
            total = total.astype(BF)
            columns = pl.ds(pl.multiple_of(n * 256, 256), 256)
            for place, j in enumerate(slots):
                pbuf[j, :, columns] = total[place * ROWS : (place + 1) * ROWS]
            return carry

        lax.fori_loop(0, 4, one, 0)

    def piece(owner):
        return pl.ds(pl.multiple_of(owner * 16, 16), 16)

    x_copies = []

    def scatter(slots):
        for j in slots:
            for place, (dx, dy) in enumerate(AROUND):
                owner = lax.rem(x + dx, 4) * 2 + lax.rem(y_lo + dy, 2)
                x_copies.append(
                    pltpu.make_async_remote_copy(
                        src_ref=pbuf.at[j, piece(owner)], dst_ref=rbuf.at[j, place],
                        send_sem=x_send, recv_sem=x_recv.at[j],
                        device_id=(ctx, owner), device_id_type=MESH,
                    )
                )
                x_copies[-1].start()

    def out_copy(j, local):
        dst = out_hbm.at[piece(ch)]
        if local:
            return pltpu.make_async_copy(sums.at[j], dst, o_recv)
        return pltpu.make_async_remote_copy(
            src_ref=sums.at[j], dst_ref=dst, send_sem=o_send, recv_sem=o_recv,
            device_id=(block_at(j) * 4 + q, z), device_id_type=MESH,
        )

    def gather(slots):
        for j in slots:
            pltpu.make_async_copy(rbuf.at[j], rbuf.at[j], x_recv.at[j]).wait()
            total = pbuf[j, piece(ch), :].astype(F32)
            for place in range(len(AROUND)):
                total = total + rbuf[j, place].astype(F32)
            sums[j] = total.astype(BF)
            if j:
                out_copy(j, False).start()
            else:
                @pl.when(is_home)
                def _():
                    out_copy(j, True).start()

                @pl.when(jnp.logical_not(is_home))
                def _():
                    out_copy(j, False).start()

    w_own.wait()
    w_across[1].wait_recv()
    w_onward[1].start()
    for part in range(2):
        w_sibling[part].wait_recv()
        w_onward[part].wait_recv()
    product(ROUNDS[0])
    scatter(ROUNDS[0])
    for r in (1, 2, 3, 4):
        a_arrive(r)
        product(ROUNDS[r])
        scatter(ROUNDS[r])
        if r >= 2:
            gather(ROUNDS[r - 2])
    gather(ROUNDS[3])
    gather(ROUNDS[4])

    for copy in (*w_across, *w_sibling, *w_onward, *a_copies.values()):
        copy.wait_send()
    pltpu.make_async_copy(rbuf, rbuf, x_send).wait()
    later = sums.at[pl.ds(1, 7)]
    pltpu.make_async_copy(later, later, o_send).wait()

    @pl.when(jnp.logical_not(is_home))
    def _():
        pltpu.make_async_copy(sums.at[0], sums.at[0], o_send).wait()

    pltpu.make_async_copy(out_hbm, out_hbm, o_recv).wait()


def shards(query_proj, key_proj, value_proj, pole_rate, residue, direct_gain, out_weight):
    vmem = pltpu.VMEM
    dma = pltpu.SemaphoreType.DMA
    block = (ROWS, WIDTH)
    grouped = (8, ROWS, 128)
    tables = (8, POLES, CHUNKS, 128)
    return pl.pallas_call(
        kernel,
        out_shape=jax.ShapeDtypeStruct(block, BF),
        in_specs=[pl.BlockSpec(memory_space=pltpu.HBM)] * 7,
        out_specs=pl.BlockSpec(memory_space=pltpu.HBM),
        scratch_shapes=[
            vmem(block, BF), vmem(block, BF), vmem(block, BF),
            vmem((POLES, WIDTH), F32), vmem((POLES, WIDTH), F32), vmem((1, WIDTH), F32),
            vmem(grouped, F32), vmem(grouped, F32), vmem(grouped, F32),
            vmem(tables, F32), vmem(tables, F32),
            vmem((CTX, 4, 128), F32),
            vmem((CTX, 4, 128), F32), vmem((CTX, 4, 128), F32),
            vmem((CTX, 4, 128), F32), vmem((CTX, 4, 128), F32),
            vmem((4, WIDTH, 256), BF), vmem((8, PARTS, ROWS, 256), BF), vmem((8, ROWS, WIDTH), BF),
            vmem((8, len(AROUND), 16, WIDTH), BF), vmem((8, 16, WIDTH), BF),
            dma((7,)), dma((3, 2)), dma((3, 2)), dma, dma, dma, dma,
            dma((8 * PARTS,)), dma((8 * PARTS,)), dma, dma((8,)), dma, dma,
        ],
        compiler_params=pltpu.CompilerParams(
            collective_id=0, has_side_effects=True, vmem_limit_bytes=48 * 1024 * 1024
        ),
        cost_estimate=pl.CostEstimate(flops=2**31, bytes_accessed=2**21, transcendentals=2**18),
    )(
        *(
            pltpu.with_memory_space_constraint(a, pltpu.HBM)
            for a in (
                query_proj, key_proj, value_proj, pole_rate, residue,
                direct_gain.reshape(1, WIDTH), out_weight,
            )
        )
    )


def solution(mesh):
    return jax.shard_map(
        shards,
        mesh=mesh,
        in_specs=(
            P("ctx", "ch"),
            P("ctx", "ch"),
            P("ctx", "ch"),
            P(None, "ch"),
            P(None, "ch"),
            P("ch"),
            P("ch", "ctx"),
        ),
        out_specs=P("ctx", "ch"),
        check_vma=False,
    )
```

```python
import jax
import jax.numpy as jnp
from jax import lax
from jax.experimental import pallas as pl
from jax.experimental.pallas import tpu as pltpu
from jax.sharding import PartitionSpec as P

MESH = pl.DeviceIdType.MESH
BF = jnp.bfloat16
F32 = jnp.float32
POLES = 16
ROWS = 128
WIDTH = 1024
CHUNKS = 8
STEPS = 16
CTX = 32
PARTS = 4
AROUND = ((2, 1), (2, 0), (1, 1), (3, 1), (1, 0), (3, 0), (0, 1))
OFFSETS = (0, -1, 1, -2, 2, -3, 3, 4)
ROUNDS = ((0,), (1, 2), (3, 4), (5, 6), (7,))


def one_minus_exp(x):
    series = 1.0 - x / 8.0
    for k in (7.0, 6.0, 5.0, 4.0, 3.0, 2.0):
        series = 1.0 - x / k * series
    return jnp.where(x < 0.125, x * series, 1.0 - jnp.exp(-x))


def spread(rows):
    return jnp.broadcast_to(rows[:, None, :], (POLES, CHUNKS, 128))


def kernel(
    q_hbm, k_hbm, v_hbm, rate_hbm, res_hbm, gain_hbm, w_hbm, out_hbm,
    qb, kb, vb, rate, res, gain, u, y, qf, before, lead,
    fsend, fgroup, dgroup, tsend, trecv, esend, entry, wbuf, abuf, pbuf,
    rbuf, sums,
    in_sem, w_send, w_recv, f_send, f_recv, t_send, t_recv, e_send, e_recv,
    a_send, a_recv, x_send, x_recv, o_send, o_recv,
):
    ctx = lax.axis_index("ctx")
    ch = lax.axis_index("ch")
    z = lax.div(ctx, 4)
    q = lax.rem(ctx, 4)
    core = lax.rem(q, 2)
    y_hi = lax.div(q, 2)
    x = lax.div(ch, 2)
    y_lo = lax.rem(ch, 2)
    sibling = ctx + 1 - 2 * core
    across = ctx + 2 - 4 * y_hi
    beyond = z * 4 + 3 - q
    up = lax.rem(ctx + 4, CTX)
    down = lax.rem(ctx + CTX - 4, CTX)

    def block_at(j):
        return lax.rem(z + OFFSETS[j] + 8, 8)

    loads = []
    for place, (src, dst) in enumerate(
        ((k_hbm, kb), (v_hbm, vb), (rate_hbm, rate), (res_hbm, res), (gain_hbm, gain), (q_hbm, qb))
    ):
        loads.append(pltpu.make_async_copy(src, dst, in_sem.at[place]))
        loads[-1].start()
    w_own = pltpu.make_async_copy(w_hbm, wbuf.at[q], in_sem.at[6])
    w_own.start()

    bar = pltpu.get_barrier_semaphore()

    def greet(c, h):
        pl.semaphore_signal(bar, inc=1, device_id=(c, h), device_id_type=MESH)

    for c in (sibling, across, beyond):
        greet(c, ch)

    def greet_z(k, carry):
        greet(lax.rem(ctx + 4 * k, CTX), ch)
        return carry

    lax.fori_loop(1, 8, greet_z, 0)
    def greet_ch(k, carry):
        greet(ctx, lax.rem(ch + k, 8))
        return carry

    lax.fori_loop(1, 8, greet_ch, 0)
    is_home = ch == z

    def greet_ends(i, carry):
        @pl.when(jnp.logical_not(jnp.logical_and(is_home, i == z)))
        def _():
            greet(i * 4 + q, z)
            greet(ch * 4 + q, i)

        return carry

    lax.fori_loop(0, 8, greet_ends, 0)
    pl.semaphore_wait(bar, jnp.where(is_home, 17 + 14, 17 + 16))

    for place in (0, 1, 2):
        loads[place].wait()
    chunk = lax.broadcasted_iota(jnp.int32, (POLES, CHUNKS, 128), 1)

    def lanes_of(g):
        return pl.ds(pl.multiple_of(g * 128, 128), 128)

    def tokens_at(p):
        return pl.ds(p, CHUNKS, stride=STEPS)

    def ending(g, carry):
        lanes = lanes_of(g)
        u[g] = kb[:, lanes].astype(F32) * vb[:, lanes].astype(F32)
        rows = rate[:, lanes]
        decay = spread(jnp.exp(-rows))
        state = jnp.zeros((POLES, CHUNKS, 128), F32)
        for p in range(STEPS):
            state = state * decay + u[g, tokens_at(p), :][None]
        for reach in (1, 2, 4):
            over = spread(jnp.exp(-rows * (STEPS * reach)))
            moved = pltpu.roll(state, reach, 1)
            state = state + jnp.where(chunk >= reach, over * moved, 0.0)
        before[g] = jnp.where(chunk >= 1, pltpu.roll(state, 1, 1), 0.0)
        fsend[lax.div(g, 4), :, lanes_of(lax.rem(g, 4))] = state[:, CHUNKS - 1, :]
        return carry

    lax.fori_loop(0, 8, ending, 0)

    f_copies = [
        pltpu.make_async_remote_copy(
            src_ref=fsend.at[half], dst_ref=fgroup.at[q], send_sem=f_send.at[place], recv_sem=f_recv.at[place],
            device_id=(target, ch), device_id_type=MESH,
        )
        for place, (half, target) in enumerate(((core, across), (1 - core, beyond), (1 - core, sibling)))
    ]
    for copy in f_copies:
        copy.start()

    def w_copy(src, slot, part, place, target):
        rows = pl.ds(part * 512, 512)
        return pltpu.make_async_remote_copy(
            src_ref=src.at[rows], dst_ref=wbuf.at[slot, rows],
            send_sem=w_send.at[place, part], recv_sem=w_recv.at[place, part],
            device_id=(target, ch), device_id_type=MESH,
        )

    w_across = [w_copy(w_hbm, q, part, 0, across) for part in range(2)]
    w_sibling = [w_copy(w_hbm, q, part, 1, sibling) for part in range(2)]
    for copy in (*w_across, *w_sibling):
        copy.start()
    fgroup[q] = fsend[core]

    for place in (3, 4, 5):
        loads[place].wait()

    def inside(g, carry):
        lanes = lanes_of(g)
        rows = rate[:, lanes]
        coef_rows = res[:, lanes] * jnp.sqrt(one_minus_exp(2.0 * rows))
        decay = spread(jnp.exp(-rows))
        coef = spread(coef_rows)
        lead[g] = coef * jnp.exp(-spread(rows) * (1.0 + STEPS * chunk.astype(F32)))
        direct = jnp.broadcast_to(gain[0:1, lanes], (CHUNKS, 128))
        qf[g] = qb[:, lanes].astype(F32)
        state = before[g]
        for p in range(STEPS):
            token = u[g, tokens_at(p), :]
            state = state * decay + token[None]
            y[g, tokens_at(p), :] = direct * token + jnp.sum(coef * state, axis=0)
        return carry

    lax.fori_loop(0, 4, inside, 0)

    for copy in f_copies:
        copy.wait_recv()
    half_rows = rate[:, pl.ds(pl.multiple_of(core * 512, 512), 512)]
    own_decay = jnp.exp(-half_rows * ROWS)
    group_decay = jnp.exp(-half_rows * (4 * ROWS))
    total = jnp.zeros((POLES, 512), F32)
    for i in range(4):
        dgroup[i] = total
        total = total * own_decay + fgroup[i]
    tsend[...] = total.astype(BF)

    def t_copy(dz):
        return pltpu.make_async_remote_copy(
            src_ref=tsend, dst_ref=trecv.at[z], send_sem=t_send.at[dz], recv_sem=t_recv.at[z],
            device_id=(lax.rem(ctx + 4 * dz, CTX), ch), device_id_type=MESH,
        )

    for dz in (4, 3, 5, 2, 6, 1, 7):
        @pl.when(z + dz < 8)
        def _():
            t_copy(dz).start()

    lax.fori_loop(4, 8, inside, 0)

    def earlier(i, so_far):
        pltpu.make_async_copy(trecv.at[i], trecv.at[i], t_recv.at[i]).wait()
        return so_far * group_decay + trecv[i].astype(F32)

    so_far = lax.fori_loop(0, z, earlier, jnp.zeros((POLES, 512), F32))

    def entry_of(place):
        return so_far * jnp.exp(-half_rows * (ROWS * place).astype(F32)) + dgroup[place]

    esend[...] = entry_of(q + 1 - 2 * core)
    e_copy = pltpu.make_async_remote_copy(
        src_ref=esend, dst_ref=entry.at[core], send_sem=e_send, recv_sem=e_recv,
        device_id=(sibling, ch), device_id_type=MESH,
    )
    e_copy.start()
    entry[core] = entry_of(q)

    def a_copy(r, way, c):
        src = 0 if r == 1 else 2 * (r - 1) - 1 + way
        dst = 7 if r == 4 else 2 * r - 1 + way
        place = ((r - 1) * 2 + way) * PARTS + c
        return pltpu.make_async_remote_copy(
            src_ref=abuf.at[src, c], dst_ref=abuf.at[dst, c],
            send_sem=a_send.at[place], recv_sem=a_recv.at[place],
            device_id=((up, down)[way], ch), device_id_type=MESH,
        )

    def finish(k, carry):
        g = lax.rem(4 * core + k, 8)
        lanes = lanes_of(g)
        decay = spread(jnp.exp(-rate[:, lanes]))
        rest = lead[g] * spread(entry[lax.div(g, 4), :, lanes_of(lax.rem(g, 4))])
        for p in range(STEPS):
            y[g, tokens_at(p), :] = qf[g, tokens_at(p), :] * (
                y[g, tokens_at(p), :] + jnp.sum(rest, axis=0)
            )
            rest = rest * decay
        abuf[0, lax.div(k, 2), :, lanes_of(lax.rem(k, 2))] = y[g].astype(BF)
        return carry

    a_copies = {}

    def a_go(r, way, c):
        a_copies[r, way, c] = a_copy(r, way, c)
        a_copies[r, way, c].start()

    order = tuple(zip((0, 2, 1, 3), (1, 3, 0, 2)))
    for c in range(PARTS):
        if c == 2:
            e_copy.wait_recv()
        lax.fori_loop(2 * c, 2 * c + 2, finish, 0)
        a_go(1, c % 2, c)
    for way, c in ((0, 1), (1, 0), (0, 3), (1, 2)):
        a_go(1, way, c)

    def a_arrive(r):
        for pair in order:
            for way, c in enumerate(pair):
                if r < 4 or way == c % 2:
                    a_copies[r, way, c].wait_recv()
                    if r < 3 or (r == 3 and way == c % 2):
                        a_go(r + 1, way, c)

    def product(slots):
        def one(n, carry):
            total = None
            for c in range(PARTS):
                left = jnp.concatenate([abuf[j, c] for j in slots], axis=0) if len(slots) > 1 else abuf[slots[0], c]
                rows = pl.ds(pl.multiple_of(lax.rem(2 * core + c, PARTS) * 256, 256), 256)
                term = jnp.dot(left, wbuf[n, rows, :], preferred_element_type=F32)
                total = term if total is None else total + term
            total = total.astype(BF)
            columns = pl.ds(pl.multiple_of(n * 256, 256), 256)
            for place, j in enumerate(slots):
                pbuf[j, :, columns] = total[place * ROWS : (place + 1) * ROWS]
            return carry

        lax.fori_loop(0, 4, one, 0)

    def piece(owner):
        return pl.ds(pl.multiple_of(owner * 16, 16), 16)

    x_copies = []

    def scatter(slots):
        for j in slots:
            for place, (dx, dy) in enumerate(AROUND):
                owner = lax.rem(x + dx, 4) * 2 + lax.rem(y_lo + dy, 2)
                x_copies.append(
                    pltpu.make_async_remote_copy(
                        src_ref=pbuf.at[j, piece(owner)], dst_ref=rbuf.at[j, place],
                        send_sem=x_send, recv_sem=x_recv.at[j],
                        device_id=(ctx, owner), device_id_type=MESH,
                    )
                )
                x_copies[-1].start()

    def out_copy(j, local):
        dst = out_hbm.at[piece(ch)]
        if local:
            return pltpu.make_async_copy(sums.at[j], dst, o_recv)
        return pltpu.make_async_remote_copy(
            src_ref=sums.at[j], dst_ref=dst, send_sem=o_send, recv_sem=o_recv,
            device_id=(block_at(j) * 4 + q, z), device_id_type=MESH,
        )

    def gather(slots):
        for j in slots:
            pltpu.make_async_copy(rbuf.at[j], rbuf.at[j], x_recv.at[j]).wait()
            total = pbuf[j, piece(ch), :].astype(F32)
            for place in range(len(AROUND)):
                total = total + rbuf[j, place].astype(F32)
            sums[j] = total.astype(BF)
            if j:
                out_copy(j, False).start()
            else:
                @pl.when(is_home)
                def _():
                    out_copy(j, True).start()

                @pl.when(jnp.logical_not(is_home))
                def _():
                    out_copy(j, False).start()

    w_own.wait()
    across_slot = lax.rem(q + 2, 4)
    w_onward = [w_copy(wbuf.at[across_slot], across_slot, part, 2, sibling) for part in range(2)]
    for part in range(2):
        w_across[part].wait_recv()
        w_onward[part].start()
    for part in range(2):
        w_sibling[part].wait_recv()
        w_onward[part].wait_recv()
    product(ROUNDS[0])
    scatter(ROUNDS[0])
    for r in (1, 2, 3, 4):
        a_arrive(r)
        product(ROUNDS[r])
        scatter(ROUNDS[r])
        if r >= 2:
            gather(ROUNDS[r - 2])
    gather(ROUNDS[3])
    gather(ROUNDS[4])

    for copy in (*f_copies, *w_across, *w_sibling, e_copy, *w_onward, *a_copies.values()):
        copy.wait_send()
    for dz in range(1, 8):
        @pl.when(z + dz < 8)
        def _():
            t_copy(dz).wait_send()

    pltpu.make_async_copy(rbuf, rbuf, x_send).wait()
    later = sums.at[pl.ds(1, 7)]
    pltpu.make_async_copy(later, later, o_send).wait()

    @pl.when(jnp.logical_not(is_home))
    def _():
        pltpu.make_async_copy(sums.at[0], sums.at[0], o_send).wait()

    pltpu.make_async_copy(out_hbm, out_hbm, o_recv).wait()


def shards(query_proj, key_proj, value_proj, pole_rate, residue, direct_gain, out_weight):
    vmem = pltpu.VMEM
    dma = pltpu.SemaphoreType.DMA
    block = (ROWS, WIDTH)
    grouped = (8, ROWS, 128)
    tables = (8, POLES, CHUNKS, 128)
    return pl.pallas_call(
        kernel,
        out_shape=jax.ShapeDtypeStruct(block, BF),
        in_specs=[pl.BlockSpec(memory_space=pltpu.HBM)] * 7,
        out_specs=pl.BlockSpec(memory_space=pltpu.HBM),
        scratch_shapes=[
            vmem(block, BF), vmem(block, BF), vmem(block, BF),
            vmem((POLES, WIDTH), F32), vmem((POLES, WIDTH), F32), vmem((1, WIDTH), F32),
            vmem(grouped, F32), vmem(grouped, F32), vmem(grouped, F32),
            vmem(tables, F32), vmem(tables, F32),
            vmem((2, POLES, 512), F32), vmem((4, POLES, 512), F32), vmem((4, POLES, 512), F32),
            vmem((POLES, 512), BF), vmem((8, POLES, 512), BF),
            vmem((POLES, 512), F32), vmem((2, POLES, 512), F32),
            vmem((4, WIDTH, 256), BF), vmem((8, PARTS, ROWS, 256), BF), vmem((8, ROWS, WIDTH), BF),
            vmem((8, len(AROUND), 16, WIDTH), BF), vmem((8, 16, WIDTH), BF),
            dma((7,)), dma((3, 2)), dma((3, 2)), dma((3,)), dma((3,)), dma((8,)), dma((8,)), dma, dma,
            dma((8 * PARTS,)), dma((8 * PARTS,)), dma, dma((8,)), dma, dma,
        ],
        compiler_params=pltpu.CompilerParams(
            collective_id=0, has_side_effects=True, vmem_limit_bytes=48 * 1024 * 1024
        ),
        cost_estimate=pl.CostEstimate(flops=2**31, bytes_accessed=2**21, transcendentals=2**18),
    )(
        *(
            pltpu.with_memory_space_constraint(a, pltpu.HBM)
            for a in (
                query_proj, key_proj, value_proj, pole_rate, residue,
                direct_gain.reshape(1, WIDTH), out_weight,
            )
        )
    )


def solution(mesh):
    return jax.shard_map(
        shards,
        mesh=mesh,
        in_specs=(
            P("ctx", "ch"),
            P("ctx", "ch"),
            P("ctx", "ch"),
            P(None, "ch"),
            P(None, "ch"),
            P("ch"),
            P("ch", "ctx"),
        ),
        out_specs=P("ctx", "ch"),
        check_vma=False,
    )
```

```python
import jax
import jax.numpy as jnp
from jax import lax
from jax.experimental import pallas as pl
from jax.experimental.pallas import tpu as pltpu
from jax.sharding import PartitionSpec as P

MESH = pl.DeviceIdType.MESH
BF = jnp.bfloat16
F32 = jnp.float32
POLES = 16
ROWS = 128
WIDTH = 1024
CHUNKS = 8
STEPS = 16
CTX = 32
PARTS = 4
AROUND = ((2, 1), (2, 0), (1, 1), (3, 1), (1, 0), (3, 0), (0, 1))
OFFSETS = (0, -1, 1, -2, 2, -3, 3, 4)
ROUNDS = ((0,), (1, 2), (3, 4), (5, 6), (7,))


def one_minus_exp(x):
    series = 1.0 - x / 8.0
    for k in (7.0, 6.0, 5.0, 4.0, 3.0, 2.0):
        series = 1.0 - x / k * series
    return jnp.where(x < 0.125, x * series, 1.0 - jnp.exp(-x))


def spread(rows):
    return jnp.broadcast_to(rows[:, None, :], (POLES, CHUNKS, 128))


def kernel(
    q_hbm, k_hbm, v_hbm, rate_hbm, res_hbm, gain_hbm, w_hbm, out_hbm,
    qb, kb, vb, rate, res, gain, u, y, qf, before, lead,
    fsend, fgroup, dgroup, tsend, trecv, esend, entry, wbuf, abuf, pbuf,
    rbuf, sums,
    in_sem, w_send, w_recv, f_send, f_recv, t_send, t_recv, e_send, e_recv,
    a_send, a_recv, x_send, x_recv, o_send, o_recv,
):
    ctx = lax.axis_index("ctx")
    ch = lax.axis_index("ch")
    z = lax.div(ctx, 4)
    q = lax.rem(ctx, 4)
    core = lax.rem(q, 2)
    y_hi = lax.div(q, 2)
    x = lax.div(ch, 2)
    y_lo = lax.rem(ch, 2)
    sibling = ctx + 1 - 2 * core
    across = ctx + 2 - 4 * y_hi
    beyond = z * 4 + 3 - q
    up = lax.rem(ctx + 4, CTX)
    down = lax.rem(ctx + CTX - 4, CTX)

    def block_at(j):
        return lax.rem(z + OFFSETS[j] + 8, 8)

    loads = []
    for place, (src, dst) in enumerate(
        ((k_hbm, kb), (v_hbm, vb), (rate_hbm, rate), (res_hbm, res), (gain_hbm, gain), (q_hbm, qb))
    ):
        loads.append(pltpu.make_async_copy(src, dst, in_sem.at[place]))
        loads[-1].start()
    w_own = pltpu.make_async_copy(w_hbm, wbuf.at[q], in_sem.at[6])
    w_own.start()

    bar = pltpu.get_barrier_semaphore()

    def greet(c, h):
        pl.semaphore_signal(bar, inc=1, device_id=(c, h), device_id_type=MESH)

    for c in (sibling, across, beyond):
        greet(c, ch)

    def greet_z(k, carry):
        greet(lax.rem(ctx + 4 * k, CTX), ch)
        return carry

    lax.fori_loop(1, 8, greet_z, 0)
    def greet_ch(k, carry):
        greet(ctx, lax.rem(ch + k, 8))
        return carry

    lax.fori_loop(1, 8, greet_ch, 0)
    is_home = ch == z

    pl.semaphore_wait(bar, 17)

    for place in (0, 1, 2):
        loads[place].wait()
    chunk = lax.broadcasted_iota(jnp.int32, (POLES, CHUNKS, 128), 1)

    def lanes_of(g):
        return pl.ds(pl.multiple_of(g * 128, 128), 128)

    def tokens_at(p):
        return pl.ds(p, CHUNKS, stride=STEPS)

    def ending(g, carry):
        lanes = lanes_of(g)
        u[g] = kb[:, lanes].astype(F32) * vb[:, lanes].astype(F32)
        rows = rate[:, lanes]
        decay = spread(jnp.exp(-rows))
        state = jnp.zeros((POLES, CHUNKS, 128), F32)
        for p in range(STEPS):
            state = state * decay + u[g, tokens_at(p), :][None]
        for reach in (1, 2, 4):
            over = spread(jnp.exp(-rows * (STEPS * reach)))
            moved = pltpu.roll(state, reach, 1)
            state = state + jnp.where(chunk >= reach, over * moved, 0.0)
        before[g] = jnp.where(chunk >= 1, pltpu.roll(state, 1, 1), 0.0)
        fsend[lax.div(g, 4), :, lanes_of(lax.rem(g, 4))] = state[:, CHUNKS - 1, :]
        return carry

    lax.fori_loop(0, 8, ending, 0)

    f_copies = [
        pltpu.make_async_remote_copy(
            src_ref=fsend.at[half], dst_ref=fgroup.at[q], send_sem=f_send.at[place], recv_sem=f_recv.at[place],
            device_id=(target, ch), device_id_type=MESH,
        )
        for place, (half, target) in enumerate(((core, across), (1 - core, beyond), (1 - core, sibling)))
    ]
    for copy in f_copies:
        copy.start()

    def w_copy(src, slot, part, place, target):
        rows = pl.ds(part * 512, 512)
        return pltpu.make_async_remote_copy(
            src_ref=src.at[rows], dst_ref=wbuf.at[slot, rows],
            send_sem=w_send.at[place, part], recv_sem=w_recv.at[place, part],
            device_id=(target, ch), device_id_type=MESH,
        )

    w_across = [w_copy(w_hbm, q, part, 0, across) for part in range(2)]
    w_sibling = [w_copy(w_hbm, q, part, 1, sibling) for part in range(2)]
    for copy in (*w_across, *w_sibling):
        copy.start()
    fgroup[q] = fsend[core]

    for place in (3, 4, 5):
        loads[place].wait()

    def inside(g, carry):
        lanes = lanes_of(g)
        rows = rate[:, lanes]
        coef_rows = res[:, lanes] * jnp.sqrt(one_minus_exp(2.0 * rows))
        decay = spread(jnp.exp(-rows))
        coef = spread(coef_rows)
        lead[g] = coef * jnp.exp(-spread(rows) * (1.0 + STEPS * chunk.astype(F32)))
        direct = jnp.broadcast_to(gain[0:1, lanes], (CHUNKS, 128))
        qf[g] = qb[:, lanes].astype(F32)
        state = before[g]
        for p in range(STEPS):
            token = u[g, tokens_at(p), :]
            state = state * decay + token[None]
            y[g, tokens_at(p), :] = direct * token + jnp.sum(coef * state, axis=0)
        return carry

    lax.fori_loop(0, 8, inside, 0)

    for copy in f_copies:
        copy.wait_recv()
    half_rows = rate[:, pl.ds(pl.multiple_of(core * 512, 512), 512)]
    own_decay = jnp.exp(-half_rows * ROWS)
    group_decay = jnp.exp(-half_rows * (4 * ROWS))
    total = jnp.zeros((POLES, 512), F32)
    for i in range(4):
        dgroup[i] = total
        total = total * own_decay + fgroup[i]
    tsend[...] = total.astype(BF)

    def t_copy(dz):
        return pltpu.make_async_remote_copy(
            src_ref=tsend, dst_ref=trecv.at[z], send_sem=t_send.at[dz], recv_sem=t_recv.at[z],
            device_id=(lax.rem(ctx + 4 * dz, CTX), ch), device_id_type=MESH,
        )

    for dz in (4, 3, 5, 2, 6, 1, 7):
        @pl.when(z + dz < 8)
        def _():
            t_copy(dz).start()

    def earlier(i, so_far):
        pltpu.make_async_copy(trecv.at[i], trecv.at[i], t_recv.at[i]).wait()
        return so_far * group_decay + trecv[i].astype(F32)

    so_far = lax.fori_loop(0, z, earlier, jnp.zeros((POLES, 512), F32))

    def entry_of(place):
        return so_far * jnp.exp(-half_rows * (ROWS * place).astype(F32)) + dgroup[place]

    esend[...] = entry_of(q + 1 - 2 * core)
    e_copy = pltpu.make_async_remote_copy(
        src_ref=esend, dst_ref=entry.at[core], send_sem=e_send, recv_sem=e_recv,
        device_id=(sibling, ch), device_id_type=MESH,
    )
    e_copy.start()
    entry[core] = entry_of(q)

    def a_copy(r, way, c):
        src = 0 if r == 1 else 2 * (r - 1) - 1 + way
        dst = 7 if r == 4 else 2 * r - 1 + way
        place = ((r - 1) * 2 + way) * PARTS + c
        return pltpu.make_async_remote_copy(
            src_ref=abuf.at[src, c], dst_ref=abuf.at[dst, c],
            send_sem=a_send.at[place], recv_sem=a_recv.at[place],
            device_id=((up, down)[way], ch), device_id_type=MESH,
        )

    def finish(k, carry):
        g = lax.rem(4 * core + k, 8)
        lanes = lanes_of(g)
        decay = spread(jnp.exp(-rate[:, lanes]))
        rest = lead[g] * spread(entry[lax.div(g, 4), :, lanes_of(lax.rem(g, 4))])
        for p in range(STEPS):
            y[g, tokens_at(p), :] = qf[g, tokens_at(p), :] * (
                y[g, tokens_at(p), :] + jnp.sum(rest, axis=0)
            )
            rest = rest * decay
        abuf[0, lax.div(k, 2), :, lanes_of(lax.rem(k, 2))] = y[g].astype(BF)
        return carry

    a_copies = {}

    def a_go(r, way, c):
        a_copies[r, way, c] = a_copy(r, way, c)
        a_copies[r, way, c].start()

    order = tuple(zip((0, 2, 1, 3), (1, 3, 0, 2)))
    for c in range(PARTS):
        if c == 2:
            e_copy.wait_recv()
        lax.fori_loop(2 * c, 2 * c + 2, finish, 0)
        a_go(1, c % 2, c)
    for way, c in ((0, 1), (1, 0), (0, 3), (1, 2)):
        a_go(1, way, c)

    def a_arrive(r):
        for pair in order:
            for way, c in enumerate(pair):
                if r < 4 or way == c % 2:
                    a_copies[r, way, c].wait_recv()
                    if r < 3 or (r == 3 and way == c % 2):
                        a_go(r + 1, way, c)

    def product(slots):
        def one(n, carry):
            total = None
            for c in range(PARTS):
                left = jnp.concatenate([abuf[j, c] for j in slots], axis=0) if len(slots) > 1 else abuf[slots[0], c]
                rows = pl.ds(pl.multiple_of(lax.rem(2 * core + c, PARTS) * 256, 256), 256)
                term = jnp.dot(left, wbuf[n, rows, :], preferred_element_type=F32)
                total = term if total is None else total + term
            total = total.astype(BF)
            columns = pl.ds(pl.multiple_of(n * 256, 256), 256)
            for place, j in enumerate(slots):
                pbuf[j, :, columns] = total[place * ROWS : (place + 1) * ROWS]
            return carry

        lax.fori_loop(0, 4, one, 0)

    def piece(owner):
        return pl.ds(pl.multiple_of(owner * 16, 16), 16)

    x_copies = []

    def scatter(slots):
        for j in slots:
            for place, (dx, dy) in enumerate(AROUND):
                owner = lax.rem(x + dx, 4) * 2 + lax.rem(y_lo + dy, 2)
                x_copies.append(
                    pltpu.make_async_remote_copy(
                        src_ref=pbuf.at[j, piece(owner)], dst_ref=rbuf.at[j, place],
                        send_sem=x_send, recv_sem=x_recv.at[j],
                        device_id=(ctx, owner), device_id_type=MESH,
                    )
                )
                x_copies[-1].start()

    def out_copy(j, local):
        dst = out_hbm.at[piece(ch)]
        if local:
            return pltpu.make_async_copy(sums.at[j], dst, o_recv)
        return pltpu.make_async_remote_copy(
            src_ref=sums.at[j], dst_ref=dst, send_sem=o_send, recv_sem=o_recv,
            device_id=(block_at(j) * 4 + q, z), device_id_type=MESH,
        )

    def gather(slots):
        for j in slots:
            pltpu.make_async_copy(rbuf.at[j], rbuf.at[j], x_recv.at[j]).wait()
            total = pbuf[j, piece(ch), :].astype(F32)
            for place in range(len(AROUND)):
                total = total + rbuf[j, place].astype(F32)
            sums[j] = total.astype(BF)
            if j:
                out_copy(j, False).start()
            else:
                @pl.when(is_home)
                def _():
                    out_copy(j, True).start()

                @pl.when(jnp.logical_not(is_home))
                def _():
                    out_copy(j, False).start()

    w_own.wait()
    across_slot = lax.rem(q + 2, 4)
    w_onward = [w_copy(wbuf.at[across_slot], across_slot, part, 2, sibling) for part in range(2)]
    for part in range(2):
        w_across[part].wait_recv()
        w_onward[part].start()
    for part in range(2):
        w_sibling[part].wait_recv()
        w_onward[part].wait_recv()
    product(ROUNDS[0])
    scatter(ROUNDS[0])
    for r in (1, 2, 3, 4):
        a_arrive(r)
        product(ROUNDS[r])
        scatter(ROUNDS[r])
        if r >= 2:
            gather(ROUNDS[r - 2])
    gather(ROUNDS[3])
    gather(ROUNDS[4])

    for copy in (*f_copies, *w_across, *w_sibling, e_copy, *w_onward, *a_copies.values()):
        copy.wait_send()
    for dz in range(1, 8):
        @pl.when(z + dz < 8)
        def _():
            t_copy(dz).wait_send()

    pltpu.make_async_copy(rbuf, rbuf, x_send).wait()
    later = sums.at[pl.ds(1, 7)]
    pltpu.make_async_copy(later, later, o_send).wait()

    @pl.when(jnp.logical_not(is_home))
    def _():
        pltpu.make_async_copy(sums.at[0], sums.at[0], o_send).wait()

    pltpu.make_async_copy(out_hbm, out_hbm, o_recv).wait()


def shards(query_proj, key_proj, value_proj, pole_rate, residue, direct_gain, out_weight):
    vmem = pltpu.VMEM
    dma = pltpu.SemaphoreType.DMA
    block = (ROWS, WIDTH)
    grouped = (8, ROWS, 128)
    tables = (8, POLES, CHUNKS, 128)
    return pl.pallas_call(
        kernel,
        out_shape=jax.ShapeDtypeStruct(block, BF),
        in_specs=[pl.BlockSpec(memory_space=pltpu.HBM)] * 7,
        out_specs=pl.BlockSpec(memory_space=pltpu.HBM),
        scratch_shapes=[
            vmem(block, BF), vmem(block, BF), vmem(block, BF),
            vmem((POLES, WIDTH), F32), vmem((POLES, WIDTH), F32), vmem((1, WIDTH), F32),
            vmem(grouped, F32), vmem(grouped, F32), vmem(grouped, F32),
            vmem(tables, F32), vmem(tables, F32),
            vmem((2, POLES, 512), F32), vmem((4, POLES, 512), F32), vmem((4, POLES, 512), F32),
            vmem((POLES, 512), BF), vmem((8, POLES, 512), BF),
            vmem((POLES, 512), F32), vmem((2, POLES, 512), F32),
            vmem((4, WIDTH, 256), BF), vmem((8, PARTS, ROWS, 256), BF), vmem((8, ROWS, WIDTH), BF),
            vmem((8, len(AROUND), 16, WIDTH), BF), vmem((8, 16, WIDTH), BF),
            dma((7,)), dma((3, 2)), dma((3, 2)), dma((3,)), dma((3,)), dma((8,)), dma((8,)), dma, dma,
            dma((8 * PARTS,)), dma((8 * PARTS,)), dma, dma((8,)), dma, dma,
        ],
        compiler_params=pltpu.CompilerParams(
            collective_id=0, has_side_effects=True, vmem_limit_bytes=48 * 1024 * 1024
        ),
        cost_estimate=pl.CostEstimate(flops=2**31, bytes_accessed=2**21, transcendentals=2**18),
    )(
        *(
            pltpu.with_memory_space_constraint(a, pltpu.HBM)
            for a in (
                query_proj, key_proj, value_proj, pole_rate, residue,
                direct_gain.reshape(1, WIDTH), out_weight,
            )
        )
    )


def solution(mesh):
    return jax.shard_map(
        shards,
        mesh=mesh,
        in_specs=(
            P("ctx", "ch"),
            P("ctx", "ch"),
            P("ctx", "ch"),
            P(None, "ch"),
            P(None, "ch"),
            P("ch"),
            P("ch", "ctx"),
        ),
        out_specs=P("ctx", "ch"),
        check_vma=False,
    )
```

```python
import jax
import jax.numpy as jnp
from jax import lax
from jax.experimental import pallas as pl
from jax.experimental.pallas import tpu as pltpu
from jax.sharding import PartitionSpec as P

MESH = pl.DeviceIdType.MESH
BF = jnp.bfloat16
F32 = jnp.float32
POLES = 16
ROWS = 128
WIDTH = 1024
CHUNKS = 8
STEPS = 16
CTX = 32
PARTS = 2
AROUND = ((2, 1), (2, 0), (1, 1), (3, 1), (1, 0), (3, 0), (0, 1))
STAGED = 7


def one_minus_exp(x):
    series = 1.0 - x / 8.0
    for k in (7.0, 6.0, 5.0, 4.0, 3.0, 2.0):
        series = 1.0 - x / k * series
    return jnp.where(x < 0.125, x * series, 1.0 - jnp.exp(-x))


def spread(rows):
    return jnp.broadcast_to(rows[:, None, :], (POLES, CHUNKS, 128))


def kernel(
    q_hbm, k_hbm, v_hbm, rate_hbm, res_hbm, gain_hbm, w_hbm, out_hbm,
    qb, kb, vb, rate, res, gain, u, y, qf, before, lead,
    fsend, fgroup, dgroup, tsend, trecv, esend, entry, wbuf, abuf,
    part, r1, p2, r2, r7, sums,
    in_sem, w_send, w_recv, f_send, f_recv, t_send, t_recv, e_send, e_recv,
    a_send, a_recv, x_send, x_recv, o_send, o_recv,
):
    ctx = lax.axis_index("ctx")
    ch = lax.axis_index("ch")
    z = lax.div(ctx, 4)
    q = lax.rem(ctx, 4)
    core = lax.rem(q, 2)
    y_hi = lax.div(q, 2)
    x = lax.div(ch, 2)
    y_lo = lax.rem(ch, 2)
    x0 = lax.rem(x, 2)
    x1 = lax.div(x, 2)
    near = lax.rem(x0 + x1, 2)
    far = x1
    near_ch = ch + 2 - 4 * x0
    far_ch = (3 - x) * 2 + y_lo
    sibling = ctx + 1 - 2 * core
    across = ctx + 2 - 4 * y_hi
    beyond = z * 4 + 3 - q
    up = lax.rem(ctx + 4, CTX)
    down = lax.rem(ctx + CTX - 4, CTX)

    loads = []
    for place, (src, dst) in enumerate(
        ((k_hbm, kb), (v_hbm, vb), (rate_hbm, rate), (res_hbm, res), (gain_hbm, gain), (q_hbm, qb))
    ):
        loads.append(pltpu.make_async_copy(src, dst, in_sem.at[place]))
        loads[-1].start()
    w_own = pltpu.make_async_copy(w_hbm, wbuf.at[q], in_sem.at[6])
    w_own.start()

    bar = pltpu.get_barrier_semaphore()

    def greet(c, h):
        pl.semaphore_signal(bar, inc=1, device_id=(c, h), device_id_type=MESH)

    for c in (sibling, across, beyond):
        greet(c, ch)

    def greet_z(k, carry):
        greet(lax.rem(ctx + 4 * k, CTX), ch)
        return carry

    lax.fori_loop(1, 8, greet_z, 0)
    def greet_ch(k, carry):
        greet(ctx, lax.rem(ch + k, 8))
        return carry

    lax.fori_loop(1, 8, greet_ch, 0)
    is_home = ch == z
    pl.semaphore_wait(bar, 17)

    for place in (0, 1, 2):
        loads[place].wait()
    chunk = lax.broadcasted_iota(jnp.int32, (POLES, CHUNKS, 128), 1)

    def lanes_of(g):
        return pl.ds(pl.multiple_of(g * 128, 128), 128)

    def half_of(c):
        return pl.ds(pl.multiple_of(c * 512, 512), 512)

    def tokens_at(p):
        return pl.ds(p, CHUNKS, stride=STEPS)

    def ending(g, carry):
        lanes = lanes_of(g)
        u[g] = kb[:, lanes].astype(F32) * vb[:, lanes].astype(F32)
        rows = rate[:, lanes]
        decay = spread(jnp.exp(-rows))
        state = jnp.zeros((POLES, CHUNKS, 128), F32)
        for p in range(STEPS):
            state = state * decay + u[g, tokens_at(p), :][None]
        for reach in (1, 2, 4):
            over = spread(jnp.exp(-rows * (STEPS * reach)))
            moved = pltpu.roll(state, reach, 1)
            state = state + jnp.where(chunk >= reach, over * moved, 0.0)
        before[g] = jnp.where(chunk >= 1, pltpu.roll(state, 1, 1), 0.0)
        fsend[lax.div(g, 4), :, lanes_of(lax.rem(g, 4))] = state[:, CHUNKS - 1, :]
        return carry

    lax.fori_loop(0, 8, ending, 0)

    f_copies = [
        pltpu.make_async_remote_copy(
            src_ref=fsend.at[half], dst_ref=fgroup.at[q], send_sem=f_send.at[place], recv_sem=f_recv.at[place],
            device_id=(target, ch), device_id_type=MESH,
        )
        for place, (half, target) in enumerate(((core, across), (1 - core, beyond), (1 - core, sibling)))
    ]
    for copy in f_copies:
        copy.start()

    def w_copy(src, slot, part, place, target):
        rows = pl.ds(part * 512, 512)
        return pltpu.make_async_remote_copy(
            src_ref=src.at[rows], dst_ref=wbuf.at[slot, rows],
            send_sem=w_send.at[place, part], recv_sem=w_recv.at[place, part],
            device_id=(target, ch), device_id_type=MESH,
        )

    w_across = [w_copy(w_hbm, q, part, 0, across) for part in range(2)]
    w_sibling = [w_copy(w_hbm, q, part, 1, sibling) for part in range(2)]
    for copy in (*w_across, *w_sibling):
        copy.start()
    fgroup[q] = fsend[core]

    for place in (3, 4, 5):
        loads[place].wait()

    def inside(g, carry):
        lanes = lanes_of(g)
        rows = rate[:, lanes]
        coef_rows = res[:, lanes] * jnp.sqrt(one_minus_exp(2.0 * rows))
        decay = spread(jnp.exp(-rows))
        coef = spread(coef_rows)
        lead[g] = coef * jnp.exp(-spread(rows) * (1.0 + STEPS * chunk.astype(F32)))
        direct = jnp.broadcast_to(gain[0:1, lanes], (CHUNKS, 128))
        qf[g] = qb[:, lanes].astype(F32)
        state = before[g]
        for p in range(STEPS):
            token = u[g, tokens_at(p), :]
            state = state * decay + token[None]
            y[g, tokens_at(p), :] = direct * token + jnp.sum(coef * state, axis=0)
        return carry

    lax.fori_loop(0, 8, inside, 0)

    for copy in f_copies:
        copy.wait_recv()
    half_rows = rate[:, half_of(core)]
    own_decay = jnp.exp(-half_rows * ROWS)
    group_decay = jnp.exp(-half_rows * (4 * ROWS))
    total = jnp.zeros((POLES, 512), F32)
    for i in range(4):
        dgroup[i] = total
        total = total * own_decay + fgroup[i]
    tsend[...] = total.astype(BF)

    def t_copy(dz):
        return pltpu.make_async_remote_copy(
            src_ref=tsend, dst_ref=trecv.at[z], send_sem=t_send.at[dz], recv_sem=t_recv.at[z],
            device_id=(lax.rem(ctx + 4 * dz, CTX), ch), device_id_type=MESH,
        )

    for dz in (4, 3, 5, 2, 6, 1, 7):
        @pl.when(z + dz < 8)
        def _():
            t_copy(dz).start()

    def earlier(i, so_far):
        pltpu.make_async_copy(trecv.at[i], trecv.at[i], t_recv.at[i]).wait()
        return so_far * group_decay + trecv[i].astype(F32)

    so_far = lax.fori_loop(0, z, earlier, jnp.zeros((POLES, 512), F32))

    def entry_of(place):
        return so_far * jnp.exp(-half_rows * (ROWS * place).astype(F32)) + dgroup[place]

    esend[...] = entry_of(q + 1 - 2 * core)
    e_copy = pltpu.make_async_remote_copy(
        src_ref=esend, dst_ref=entry.at[core], send_sem=e_send, recv_sem=e_recv,
        device_id=(sibling, ch), device_id_type=MESH,
    )
    e_copy.start()
    entry[core] = entry_of(q)

    def a_copy(r, way, c):
        src = 0 if r == 1 else 2 * (r - 1) - 1 + way
        dst = 7 if r == 4 else 2 * r - 1 + way
        place = ((r - 1) * 2 + way) * PARTS + c
        return pltpu.make_async_remote_copy(
            src_ref=abuf.at[src, pl.ds(c * 64, 64)], dst_ref=abuf.at[dst, pl.ds(c * 64, 64)],
            send_sem=a_send.at[place], recv_sem=a_recv.at[place],
            device_id=((up, down)[way], ch), device_id_type=MESH,
        )

    def finish(k, carry):
        g = lax.rem(4 * core + k, 8)
        lanes = lanes_of(g)
        decay = spread(jnp.exp(-rate[:, lanes]))
        rest = lead[g] * spread(entry[lax.div(g, 4), :, lanes_of(lax.rem(g, 4))])
        for p in range(STEPS):
            y[g, tokens_at(p), :] = qf[g, tokens_at(p), :] * (
                y[g, tokens_at(p), :] + jnp.sum(rest, axis=0)
            )
            rest = rest * decay
        abuf[0, :, lanes] = y[g].astype(BF)
        return carry

    a_copies = {}

    def a_go(r, way, c):
        a_copies[r, way, c] = a_copy(r, way, c)
        a_copies[r, way, c].start()

    lax.fori_loop(0, 4, finish, 0)
    e_copy.wait_recv()
    lax.fori_loop(4, 8, finish, 0)
    for way, c in ((0, 0), (1, 1), (0, 1), (1, 0)):
        a_go(1, way, c)

    def a_arrive(r, i):
        for way in range(2):
            c = (way + i) % 2
            a_copies[r, way, c].wait_recv()
            if r < 3 or (r == 3 and i == 0):
                a_go(r + 1, way, c)

    def product(left, side, store):
        def one(h, carry):
            total = jnp.dot(left(), wbuf[2 * side + h], preferred_element_type=F32)
            store(pl.ds(pl.multiple_of(h * 256, 256), 256), total.astype(BF))
            return carry

        lax.fori_loop(0, 2, one, 0)

    def rows_at(start, size):
        return pl.ds(pl.multiple_of(start, size), size)

    def first_bit(s):
        return near + s * (far - near)

    def second_bit(s):
        return far + s * (near - far)

    def first_ch(s):
        return near_ch + s * (far_ch - near_ch)

    def second_ch(s):
        return far_ch + s * (near_ch - far_ch)

    def runs_of(t):
        if t in (0, 7):
            return ((t, 0), (t, 64))
        r, second = (t + 1) // 2, (t + 1) % 2
        return ((2 * r - 1, 64 * second), (2 * r, 64 - 64 * second))

    def place_of(t, run):
        if t in (0, 7):
            return t // 7 * 4, 64 * run
        r, second = (t + 1) // 2, (t + 1) % 2
        return r * (2 * run - 1), (64 - 64 * run if second else 64 * run)

    def multiply(t, s):
        def left():
            return jnp.concatenate([abuf[j, row : row + 64] for j, row in runs_of(t)], axis=0)

        def store(columns, total):
            for run in range(2):
                part[t, run, s, :, columns] = total[run * 64 : (run + 1) * 64]

        product(left, s, store)

    def halves(t, s):
        multiply(t, s)
        pltpu.make_async_remote_copy(
            src_ref=part.at[t, 1 - first_bit(s), s], dst_ref=r1.at[t, s],
            send_sem=x_send.at[0], recv_sem=x_recv.at[t, s],
            device_id=(ctx, first_ch(s)), device_id_type=MESH,
        ).start()

    def quarters(t):
        for s in range(2):
            pltpu.make_async_copy(r1.at[t, s], r1.at[t, s], x_recv.at[t, s]).wait()
            p2[t, s] = (part[t, first_bit(s), s].astype(F32) + r1[t, s].astype(F32)).astype(BF)
            for place, (turn, y_turn) in enumerate(((1, 1), (1, 0), (0, 1))):
                bit = 1 - second_bit(s) if turn else second_bit(s)
                y_bit = 1 - y_lo if y_turn else y_lo
                target = second_ch(s) if turn else ch
                pltpu.make_async_remote_copy(
                    src_ref=p2.at[t, s, rows_at(bit * 32 + y_bit * 16, 16)], dst_ref=r2.at[t, s, place],
                    send_sem=x_send.at[1], recv_sem=x_recv.at[8 + t, s],
                    device_id=(ctx, target - y_lo + y_bit), device_id_type=MESH,
                ).start()

    def whole(t):
        for s in range(2):
            pltpu.make_async_copy(r2.at[t, s], r2.at[t, s], x_recv.at[8 + t, s]).wait()
            row = second_bit(s) * 32 + y_lo * 16
            total = p2[t, s, rows_at(row, 16), :].astype(F32)
            for place in range(3):
                total = total + r2[t, s, place].astype(F32)
            sums[t, s] = total.astype(BF)
            steps, start = place_of(t, first_bit(s))
            place_out(sums.at[t, s], steps, start + row, s, t == 0)

    def direct(t):
        multiply(t, 0)
        multiply(t, 1)
        for place, (dx, dy) in enumerate(AROUND):
            owner_x, owner_y = lax.rem(x + dx, 4), lax.rem(y_lo + dy, 2)
            pltpu.make_async_remote_copy(
                src_ref=part.at[t, :, owner_y, rows_at(owner_x * 16, 16)], dst_ref=r7.at[t - STAGED, place],
                send_sem=x_send.at[2], recv_sem=x_recv.at[8 + t, 0],
                device_id=(ctx, owner_x * 2 + owner_y), device_id_type=MESH,
            ).start()

    def direct_whole(t):
        came = r7.at[t - STAGED]
        pltpu.make_async_copy(came, came, x_recv.at[8 + t, 0]).wait()
        total = part[t, :, y_lo, rows_at(x * 16, 16), :].astype(F32)
        for place in range(len(AROUND)):
            total = total + r7[t - STAGED, place].astype(F32)
        sums[t] = total.astype(BF)
        for run in range(2):
            steps, start = place_of(t, run)
            place_out(sums.at[t, run], steps, start + x * 16, y_lo)

    def place_out(src, steps, row, s, own=False):
        dst = out_hbm.at[rows_at(row, 16), half_of(s)]
        block = lax.rem(z + steps + 8, 8)
        remote = pltpu.make_async_remote_copy(
            src_ref=src, dst_ref=dst, send_sem=o_send, recv_sem=o_recv,
            device_id=(block * 4 + q, z), device_id_type=MESH,
        )
        if own:
            @pl.when(is_home)
            def _():
                pltpu.make_async_copy(src, dst, o_recv).start()

            @pl.when(jnp.logical_not(is_home))
            def _():
                remote.start()
        else:
            remote.start()

    across_slot = lax.rem(q + 2, 4)
    w_onward = [w_copy(wbuf.at[across_slot], across_slot, part, 2, sibling) for part in range(2)]
    w_own.wait()
    for n in range(2):
        w_sibling[n].wait_recv()
    halves(0, y_hi)
    for n in range(2):
        w_across[n].wait_recv()
        w_onward[n].start()
    for n in range(2):
        w_onward[n].wait_recv()
    halves(0, 1 - y_hi)
    a_arrive(1, 0)
    halves(1, 0)
    halves(1, 1)
    a_arrive(1, 1)
    halves(2, 0)
    halves(2, 1)
    quarters(0)
    a_arrive(2, 0)
    halves(3, 0)
    halves(3, 1)
    quarters(1)
    a_arrive(2, 1)
    halves(4, 0)
    halves(4, 1)
    quarters(2)
    whole(0)
    a_arrive(3, 0)
    halves(5, 0)
    halves(5, 1)
    quarters(3)
    whole(1)
    a_arrive(3, 1)
    halves(6, 0)
    halves(6, 1)
    quarters(4)
    whole(2)
    quarters(5)
    a_arrive(4, 0)
    direct(7)
    whole(3)
    quarters(6)
    whole(4)
    whole(5)
    direct_whole(7)
    whole(6)

    for copy in (*f_copies, *w_across, *w_sibling, e_copy, *w_onward, *a_copies.values()):
        copy.wait_send()
    for dz in range(1, 8):
        @pl.when(z + dz < 8)
        def _():
            t_copy(dz).wait_send()

    pltpu.make_async_copy(r1, r1, x_send.at[0]).wait()
    pltpu.make_async_copy(r2, r2, x_send.at[1]).wait()
    pltpu.make_async_copy(r7, r7, x_send.at[2]).wait()
    later = sums.at[pl.ds(1, 7)]
    pltpu.make_async_copy(later, later, o_send).wait()

    @pl.when(jnp.logical_not(is_home))
    def _():
        pltpu.make_async_copy(sums.at[0], sums.at[0], o_send).wait()

    pltpu.make_async_copy(out_hbm, out_hbm, o_recv).wait()


def shards(query_proj, key_proj, value_proj, pole_rate, residue, direct_gain, out_weight):
    vmem = pltpu.VMEM
    dma = pltpu.SemaphoreType.DMA
    block = (ROWS, WIDTH)
    grouped = (8, ROWS, 128)
    tables = (8, POLES, CHUNKS, 128)
    return pl.pallas_call(
        kernel,
        out_shape=jax.ShapeDtypeStruct(block, BF),
        in_specs=[pl.BlockSpec(memory_space=pltpu.HBM)] * 7,
        out_specs=pl.BlockSpec(memory_space=pltpu.HBM),
        scratch_shapes=[
            vmem(block, BF), vmem(block, BF), vmem(block, BF),
            vmem((POLES, WIDTH), F32), vmem((POLES, WIDTH), F32), vmem((1, WIDTH), F32),
            vmem(grouped, F32), vmem(grouped, F32), vmem(grouped, F32),
            vmem(tables, F32), vmem(tables, F32),
            vmem((2, POLES, 512), F32), vmem((4, POLES, 512), F32), vmem((4, POLES, 512), F32),
            vmem((POLES, 512), BF), vmem((8, POLES, 512), BF),
            vmem((POLES, 512), F32), vmem((2, POLES, 512), F32),
            vmem((4, WIDTH, 256), BF), vmem((8, ROWS, WIDTH), BF), vmem((8, 2, 2, 64, 512), BF),
            vmem((STAGED, 2, 64, 512), BF), vmem((STAGED, 2, 64, 512), BF), vmem((STAGED, 2, 3, 16, 512), BF),
            vmem((8 - STAGED, len(AROUND), 2, 16, 512), BF), vmem((8, 2, 16, 512), BF),
            dma((7,)), dma((3, 2)), dma((3, 2)), dma((3,)), dma((3,)), dma((8,)), dma((8,)), dma, dma,
            dma((8 * PARTS,)), dma((8 * PARTS,)), dma((3,)), dma((16, 2)), dma, dma,
        ],
        compiler_params=pltpu.CompilerParams(
            collective_id=0, has_side_effects=True, vmem_limit_bytes=48 * 1024 * 1024
        ),
        cost_estimate=pl.CostEstimate(flops=2**31, bytes_accessed=2**21, transcendentals=2**18),
    )(
        *(
            pltpu.with_memory_space_constraint(a, pltpu.HBM)
            for a in (
                query_proj, key_proj, value_proj, pole_rate, residue,
                direct_gain.reshape(1, WIDTH), out_weight,
            )
        )
    )


def solution(mesh):
    return jax.shard_map(
        shards,
        mesh=mesh,
        in_specs=(
            P("ctx", "ch"),
            P("ctx", "ch"),
            P("ctx", "ch"),
            P(None, "ch"),
            P(None, "ch"),
            P("ch"),
            P("ch", "ctx"),
        ),
        out_specs=P("ctx", "ch"),
        check_vma=False,
    )
```

```python
import jax
import jax.numpy as jnp
from jax import lax
from jax.experimental import pallas as pl
from jax.experimental.pallas import tpu as pltpu
from jax.sharding import PartitionSpec as P

MESH = pl.DeviceIdType.MESH
BF = jnp.bfloat16
F32 = jnp.float32
POLES = 16
ROWS = 128
WIDTH = 1024
CHUNKS = 8
STEPS = 16
CTX = 32
PARTS = 2
AROUND = ((2, 1), (2, 0), (1, 1), (3, 1), (1, 0), (3, 0), (0, 1))
STAGED = 7


def one_minus_exp(x):
    series = 1.0 - x / 8.0
    for k in (7.0, 6.0, 5.0, 4.0, 3.0, 2.0):
        series = 1.0 - x / k * series
    return jnp.where(x < 0.125, x * series, 1.0 - jnp.exp(-x))


def spread(rows):
    return jnp.broadcast_to(rows[:, None, :], (POLES, CHUNKS, 128))


def kernel(
    q_hbm, k_hbm, v_hbm, rate_hbm, res_hbm, gain_hbm, w_hbm, out_hbm,
    qb, kb, vb, rate, res, gain, u, y, qf, before, lead,
    fsend, fgroup, dgroup, tsend, trecv, esend, entry, wbuf, abuf,
    part, r1, p2, r2, r7, sums,
    in_sem, w_send, w_recv, f_send, f_recv, t_send, t_recv, e_send, e_recv,
    a_send, a_recv, x_send, x_recv, o_send, o_recv,
):
    ctx = lax.axis_index("ctx")
    ch = lax.axis_index("ch")
    z = lax.div(ctx, 4)
    q = lax.rem(ctx, 4)
    core = lax.rem(q, 2)
    y_hi = lax.div(q, 2)
    x = lax.div(ch, 2)
    y_lo = lax.rem(ch, 2)
    x0 = lax.rem(x, 2)
    x1 = lax.div(x, 2)
    near = lax.rem(x0 + x1, 2)
    far = x1
    near_ch = ch + 2 - 4 * x0
    far_ch = (3 - x) * 2 + y_lo
    sibling = ctx + 1 - 2 * core
    across = ctx + 2 - 4 * y_hi
    beyond = z * 4 + 3 - q
    up = lax.rem(ctx + 4, CTX)
    down = lax.rem(ctx + CTX - 4, CTX)

    loads = []
    for place, (src, dst) in enumerate(
        ((k_hbm, kb), (v_hbm, vb), (rate_hbm, rate), (res_hbm, res), (gain_hbm, gain), (q_hbm, qb))
    ):
        loads.append(pltpu.make_async_copy(src, dst, in_sem.at[place]))
        loads[-1].start()
    w_own = pltpu.make_async_copy(w_hbm, wbuf.at[q], in_sem.at[6])
    w_own.start()

    bar = pltpu.get_barrier_semaphore()

    def greet(c, h):
        pl.semaphore_signal(bar, inc=1, device_id=(c, h), device_id_type=MESH)

    for c in (sibling, across, beyond):
        greet(c, ch)

    def greet_z(k, carry):
        greet(lax.rem(ctx + 4 * k, CTX), ch)
        return carry

    lax.fori_loop(1, 8, greet_z, 0)
    def greet_ch(k, carry):
        greet(ctx, lax.rem(ch + k, 8))
        return carry

    lax.fori_loop(1, 8, greet_ch, 0)
    is_home = ch == z
    pl.semaphore_wait(bar, 17)

    for place in (0, 1, 2):
        loads[place].wait()
    chunk = lax.broadcasted_iota(jnp.int32, (POLES, CHUNKS, 128), 1)

    def lanes_of(g):
        return pl.ds(pl.multiple_of(g * 128, 128), 128)

    def half_of(c):
        return pl.ds(pl.multiple_of(c * 512, 512), 512)

    def tokens_at(p):
        return pl.ds(p, CHUNKS, stride=STEPS)

    def ending(g, carry):
        lanes = lanes_of(g)
        u[g] = kb[:, lanes].astype(F32) * vb[:, lanes].astype(F32)
        rows = rate[:, lanes]
        decay = spread(jnp.exp(-rows))
        state = jnp.zeros((POLES, CHUNKS, 128), F32)
        for p in range(STEPS):
            state = state * decay + u[g, tokens_at(p), :][None]
        for reach in (1, 2, 4):
            over = spread(jnp.exp(-rows * (STEPS * reach)))
            moved = pltpu.roll(state, reach, 1)
            state = state + jnp.where(chunk >= reach, over * moved, 0.0)
        before[g] = jnp.where(chunk >= 1, pltpu.roll(state, 1, 1), 0.0)
        fsend[lax.div(g, 4), :, lanes_of(lax.rem(g, 4))] = state[:, CHUNKS - 1, :]
        return carry

    lax.fori_loop(0, 8, ending, 0)

    f_copies = [
        pltpu.make_async_remote_copy(
            src_ref=fsend.at[half], dst_ref=fgroup.at[q], send_sem=f_send.at[place], recv_sem=f_recv.at[place],
            device_id=(target, ch), device_id_type=MESH,
        )
        for place, (half, target) in enumerate(((core, across), (1 - core, beyond), (1 - core, sibling)))
    ]
    for copy in f_copies:
        copy.start()

    def w_copy(src, slot, part, place, target):
        rows = pl.ds(part * 1024, 1024)
        return pltpu.make_async_remote_copy(
            src_ref=src.at[rows], dst_ref=wbuf.at[slot, rows],
            send_sem=w_send.at[place, part], recv_sem=w_recv.at[place, part],
            device_id=(target, ch), device_id_type=MESH,
        )

    w_across = [w_copy(w_hbm, q, part, 0, across) for part in range(1)]
    w_sibling = [w_copy(w_hbm, q, part, 1, sibling) for part in range(1)]
    for copy in (*w_across, *w_sibling):
        copy.start()
    fgroup[q] = fsend[core]

    for place in (3, 4, 5):
        loads[place].wait()

    def inside(g, carry):
        lanes = lanes_of(g)
        rows = rate[:, lanes]
        coef_rows = res[:, lanes] * jnp.sqrt(one_minus_exp(2.0 * rows))
        decay = spread(jnp.exp(-rows))
        coef = spread(coef_rows)
        lead[g] = coef * jnp.exp(-spread(rows) * (1.0 + STEPS * chunk.astype(F32)))
        direct = jnp.broadcast_to(gain[0:1, lanes], (CHUNKS, 128))
        qf[g] = qb[:, lanes].astype(F32)
        state = before[g]
        for p in range(STEPS):
            token = u[g, tokens_at(p), :]
            state = state * decay + token[None]
            y[g, tokens_at(p), :] = direct * token + jnp.sum(coef * state, axis=0)
        return carry

    lax.fori_loop(0, 8, inside, 0)

    for copy in f_copies:
        copy.wait_recv()
    half_rows = rate[:, half_of(core)]
    own_decay = jnp.exp(-half_rows * ROWS)
    group_decay = jnp.exp(-half_rows * (4 * ROWS))
    total = jnp.zeros((POLES, 512), F32)
    for i in range(4):
        dgroup[i] = total
        total = total * own_decay + fgroup[i]
    tsend[...] = total.astype(BF)

    def t_copy(dz):
        return pltpu.make_async_remote_copy(
            src_ref=tsend, dst_ref=trecv.at[z], send_sem=t_send.at[dz], recv_sem=t_recv.at[z],
            device_id=(lax.rem(ctx + 4 * dz, CTX), ch), device_id_type=MESH,
        )

    for dz in (4, 3, 5, 2, 6, 1, 7):
        @pl.when(z + dz < 8)
        def _():
            t_copy(dz).start()

    def earlier(i, so_far):
        pltpu.make_async_copy(trecv.at[i], trecv.at[i], t_recv.at[i]).wait()
        return so_far * group_decay + trecv[i].astype(F32)

    so_far = lax.fori_loop(0, z, earlier, jnp.zeros((POLES, 512), F32))

    def entry_of(place):
        return so_far * jnp.exp(-half_rows * (ROWS * place).astype(F32)) + dgroup[place]

    esend[...] = entry_of(q + 1 - 2 * core)
    e_copy = pltpu.make_async_remote_copy(
        src_ref=esend, dst_ref=entry.at[core], send_sem=e_send, recv_sem=e_recv,
        device_id=(sibling, ch), device_id_type=MESH,
    )
    e_copy.start()
    entry[core] = entry_of(q)

    def a_copy(r, way, c):
        src = 0 if r == 1 else 2 * (r - 1) - 1 + way
        dst = 7 if r == 4 else 2 * r - 1 + way
        place = ((r - 1) * 2 + way) * PARTS + c
        return pltpu.make_async_remote_copy(
            src_ref=abuf.at[src, pl.ds(c * 64, 64)], dst_ref=abuf.at[dst, pl.ds(c * 64, 64)],
            send_sem=a_send.at[place], recv_sem=a_recv.at[place],
            device_id=((up, down)[way], ch), device_id_type=MESH,
        )

    def finish(k, carry):
        g = lax.rem(4 * core + k, 8)
        lanes = lanes_of(g)
        decay = spread(jnp.exp(-rate[:, lanes]))
        rest = lead[g] * spread(entry[lax.div(g, 4), :, lanes_of(lax.rem(g, 4))])
        for p in range(STEPS):
            y[g, tokens_at(p), :] = qf[g, tokens_at(p), :] * (
                y[g, tokens_at(p), :] + jnp.sum(rest, axis=0)
            )
            rest = rest * decay
        abuf[0, :, lanes] = y[g].astype(BF)
        return carry

    a_copies = {}

    def a_go(r, way, c):
        a_copies[r, way, c] = a_copy(r, way, c)
        a_copies[r, way, c].start()

    def a_first(way, h):
        lanes = half_of(lax.rem(core + h, 2))
        place = 8 * PARTS + 2 * way + h
        return pltpu.make_async_remote_copy(
            src_ref=abuf.at[0, pl.ds(way * 64, 64), lanes], dst_ref=abuf.at[1 + way, pl.ds(way * 64, 64), lanes],
            send_sem=a_send.at[place], recv_sem=a_recv.at[place],
            device_id=((up, down)[way], ch), device_id_type=MESH,
        )

    firsts = [[a_first(way, h) for h in range(2)] for way in range(2)]
    lax.fori_loop(0, 4, finish, 0)
    for way in range(2):
        firsts[way][0].start()
    e_copy.wait_recv()
    lax.fori_loop(4, 8, finish, 0)
    for way in range(2):
        firsts[way][1].start()
    for way in range(2):
        a_go(1, way, 1 - way)

    def a_arrive(r, i):
        for way in range(2):
            c = (way + i) % 2
            for copy in firsts[way] if r == 1 and i == 0 else (a_copies[r, way, c],):
                copy.wait_recv()
            if r < 3 or (r == 3 and i == 0):
                a_go(r + 1, way, c)

    def product(left, side, store):
        def one(h, carry):
            total = jnp.dot(left(), wbuf[2 * side + h], preferred_element_type=F32)
            store(pl.ds(pl.multiple_of(h * 256, 256), 256), total.astype(BF))
            return carry

        lax.fori_loop(0, 2, one, 0)

    def rows_at(start, size):
        return pl.ds(pl.multiple_of(start, size), size)

    def first_bit(s):
        return near + s * (far - near)

    def second_bit(s):
        return far + s * (near - far)

    def first_ch(s):
        return near_ch + s * (far_ch - near_ch)

    def second_ch(s):
        return far_ch + s * (near_ch - far_ch)

    def runs_of(t):
        if t in (0, 7):
            return ((t, 0), (t, 64))
        r, second = (t + 1) // 2, (t + 1) % 2
        return ((2 * r - 1, 64 * second), (2 * r, 64 - 64 * second))

    def place_of(t, run):
        if t in (0, 7):
            return t // 7 * 4, 64 * run
        r, second = (t + 1) // 2, (t + 1) % 2
        return r * (2 * run - 1), (64 - 64 * run if second else 64 * run)

    def multiply(t, s):
        def left():
            return jnp.concatenate([abuf[j, row : row + 64] for j, row in runs_of(t)], axis=0)

        def store(columns, total):
            for run in range(2):
                part[t, run, s, :, columns] = total[run * 64 : (run + 1) * 64]

        product(left, s, store)

    def halves(t, s):
        multiply(t, s)
        pltpu.make_async_remote_copy(
            src_ref=part.at[t, 1 - first_bit(s), s], dst_ref=r1.at[t, s],
            send_sem=x_send.at[0], recv_sem=x_recv.at[t, s],
            device_id=(ctx, first_ch(s)), device_id_type=MESH,
        ).start()

    def quarters(t):
        for s in range(2):
            pltpu.make_async_copy(r1.at[t, s], r1.at[t, s], x_recv.at[t, s]).wait()
            p2[t, s] = (part[t, first_bit(s), s].astype(F32) + r1[t, s].astype(F32)).astype(BF)
            for place, (turn, y_turn) in enumerate(((1, 1), (1, 0), (0, 1))):
                bit = 1 - second_bit(s) if turn else second_bit(s)
                y_bit = 1 - y_lo if y_turn else y_lo
                target = second_ch(s) if turn else ch
                pltpu.make_async_remote_copy(
                    src_ref=p2.at[t, s, rows_at(bit * 32 + y_bit * 16, 16)], dst_ref=r2.at[t, s, place],
                    send_sem=x_send.at[1], recv_sem=x_recv.at[8 + t, s],
                    device_id=(ctx, target - y_lo + y_bit), device_id_type=MESH,
                ).start()

    def whole(t):
        for s in range(2):
            pltpu.make_async_copy(r2.at[t, s], r2.at[t, s], x_recv.at[8 + t, s]).wait()
            row = second_bit(s) * 32 + y_lo * 16
            total = p2[t, s, rows_at(row, 16), :].astype(F32)
            for place in range(3):
                total = total + r2[t, s, place].astype(F32)
            sums[t, s] = total.astype(BF)
            steps, start = place_of(t, first_bit(s))
            place_out(sums.at[t, s], steps, start + row, s, t == 0)

    def direct(t):
        for dy in (1, 0):
            owner_y = lax.rem(y_lo + dy, 2)
            multiply(t, owner_y)
            for place, (dx, turn) in enumerate(AROUND):
                if turn == dy:
                    owner_x = lax.rem(x + dx, 4)
                    pltpu.make_async_remote_copy(
                        src_ref=part.at[t, :, owner_y, rows_at(owner_x * 16, 16)], dst_ref=r7.at[t - STAGED, place],
                        send_sem=x_send.at[2], recv_sem=x_recv.at[8 + t, 0],
                        device_id=(ctx, owner_x * 2 + owner_y), device_id_type=MESH,
                    ).start()

    def direct_whole(t):
        came = r7.at[t - STAGED]
        pltpu.make_async_copy(came, came, x_recv.at[8 + t, 0]).wait()
        total = part[t, :, y_lo, rows_at(x * 16, 16), :].astype(F32)
        for place in range(len(AROUND)):
            total = total + r7[t - STAGED, place].astype(F32)
        sums[t] = total.astype(BF)
        for run in range(2):
            steps, start = place_of(t, run)
            place_out(sums.at[t, run], steps, start + x * 16, y_lo)

    def place_out(src, steps, row, s, own=False):
        dst = out_hbm.at[rows_at(row, 16), half_of(s)]
        block = lax.rem(z + steps + 8, 8)
        remote = pltpu.make_async_remote_copy(
            src_ref=src, dst_ref=dst, send_sem=o_send, recv_sem=o_recv,
            device_id=(block * 4 + q, z), device_id_type=MESH,
        )
        if own:
            @pl.when(is_home)
            def _():
                pltpu.make_async_copy(src, dst, o_recv).start()

            @pl.when(jnp.logical_not(is_home))
            def _():
                remote.start()
        else:
            remote.start()

    across_slot = lax.rem(q + 2, 4)
    w_onward = [w_copy(wbuf.at[across_slot], across_slot, part, 2, sibling) for part in range(1)]
    w_own.wait()
    for n in range(1):
        w_sibling[n].wait_recv()
    halves(0, y_hi)
    for n in range(1):
        w_across[n].wait_recv()
        w_onward[n].start()
    a_arrive(1, 0)
    for n in range(1):
        w_onward[n].wait_recv()
    halves(0, 1 - y_hi)
    halves(1, 0)
    halves(1, 1)
    a_arrive(1, 1)
    halves(2, 0)
    halves(2, 1)
    quarters(0)
    a_arrive(2, 0)
    quarters(1)
    halves(3, 0)
    halves(3, 1)
    a_arrive(2, 1)
    quarters(2)
    halves(4, 0)
    halves(4, 1)
    whole(0)
    a_arrive(3, 0)
    quarters(3)
    halves(5, 0)
    halves(5, 1)
    whole(1)
    a_arrive(3, 1)
    quarters(4)
    halves(6, 0)
    halves(6, 1)
    whole(2)
    quarters(5)
    a_arrive(4, 0)
    direct(7)
    quarters(6)
    whole(3)
    whole(4)
    whole(5)
    direct_whole(7)
    whole(6)

    for copy in (*f_copies, *w_across, *w_sibling, e_copy, *w_onward, *firsts[0], *firsts[1], *a_copies.values()):
        copy.wait_send()
    for dz in range(1, 8):
        @pl.when(z + dz < 8)
        def _():
            t_copy(dz).wait_send()

    pltpu.make_async_copy(r1, r1, x_send.at[0]).wait()
    pltpu.make_async_copy(r2, r2, x_send.at[1]).wait()
    pltpu.make_async_copy(r7, r7, x_send.at[2]).wait()
    later = sums.at[pl.ds(1, 7)]
    pltpu.make_async_copy(later, later, o_send).wait()

    @pl.when(jnp.logical_not(is_home))
    def _():
        pltpu.make_async_copy(sums.at[0], sums.at[0], o_send).wait()

    pltpu.make_async_copy(out_hbm, out_hbm, o_recv).wait()


def shards(query_proj, key_proj, value_proj, pole_rate, residue, direct_gain, out_weight):
    vmem = pltpu.VMEM
    dma = pltpu.SemaphoreType.DMA
    block = (ROWS, WIDTH)
    grouped = (8, ROWS, 128)
    tables = (8, POLES, CHUNKS, 128)
    return pl.pallas_call(
        kernel,
        out_shape=jax.ShapeDtypeStruct(block, BF),
        in_specs=[pl.BlockSpec(memory_space=pltpu.HBM)] * 7,
        out_specs=pl.BlockSpec(memory_space=pltpu.HBM),
        scratch_shapes=[
            vmem(block, BF), vmem(block, BF), vmem(block, BF),
            vmem((POLES, WIDTH), F32), vmem((POLES, WIDTH), F32), vmem((1, WIDTH), F32),
            vmem(grouped, F32), vmem(grouped, F32), vmem(grouped, F32),
            vmem(tables, F32), vmem(tables, F32),
            vmem((2, POLES, 512), F32), vmem((4, POLES, 512), F32), vmem((4, POLES, 512), F32),
            vmem((POLES, 512), BF), vmem((8, POLES, 512), BF),
            vmem((POLES, 512), F32), vmem((2, POLES, 512), F32),
            vmem((4, WIDTH, 256), BF), vmem((8, ROWS, WIDTH), BF), vmem((8, 2, 2, 64, 512), BF),
            vmem((STAGED, 2, 64, 512), BF), vmem((STAGED, 2, 64, 512), BF), vmem((STAGED, 2, 3, 16, 512), BF),
            vmem((8 - STAGED, len(AROUND), 2, 16, 512), BF), vmem((8, 2, 16, 512), BF),
            dma((7,)), dma((3, 2)), dma((3, 2)), dma((3,)), dma((3,)), dma((8,)), dma((8,)), dma, dma,
            dma((8 * PARTS + 4,)), dma((8 * PARTS + 4,)), dma((3,)), dma((16, 2)), dma, dma,
        ],
        compiler_params=pltpu.CompilerParams(
            collective_id=0, has_side_effects=True, vmem_limit_bytes=48 * 1024 * 1024
        ),
        cost_estimate=pl.CostEstimate(flops=2**31, bytes_accessed=2**21, transcendentals=2**18),
    )(
        *(
            pltpu.with_memory_space_constraint(a, pltpu.HBM)
            for a in (
                query_proj, key_proj, value_proj, pole_rate, residue,
                direct_gain.reshape(1, WIDTH), out_weight,
            )
        )
    )


def solution(mesh):
    return jax.shard_map(
        shards,
        mesh=mesh,
        in_specs=(
            P("ctx", "ch"),
            P("ctx", "ch"),
            P("ctx", "ch"),
            P(None, "ch"),
            P(None, "ch"),
            P("ch"),
            P("ch", "ctx"),
        ),
        out_specs=P("ctx", "ch"),
        check_vma=False,
    )
```

```python
import jax
import jax.numpy as jnp
from jax import lax
from jax.experimental import pallas as pl
from jax.experimental.pallas import tpu as pltpu
from jax.sharding import PartitionSpec as P

MESH = pl.DeviceIdType.MESH
BF = jnp.bfloat16
F32 = jnp.float32
POLES = 16
ROWS = 128
WIDTH = 1024
CHUNKS = 8
STEPS = 16
CTX = 32
PARTS = 2
AROUND = ((2, 1), (2, 0), (1, 1), (3, 1), (1, 0), (3, 0), (0, 1))
STAGED = 7


def one_minus_exp(x):
    series = 1.0 - x / 8.0
    for k in (7.0, 6.0, 5.0, 4.0, 3.0, 2.0):
        series = 1.0 - x / k * series
    return jnp.where(x < 0.125, x * series, 1.0 - jnp.exp(-x))


def spread(rows):
    return jnp.broadcast_to(rows[:, None, :], (POLES, CHUNKS, 128))


def kernel(
    q_hbm, k_hbm, v_hbm, rate_hbm, res_hbm, gain_hbm, w_hbm, out_hbm,
    qb, kb, vb, rate, res, gain, u, y, qf, before, lead,
    fsend, fgroup, dgroup, tsend, trecv, esend, entry, wbuf, abuf,
    part, r1, p2, r2, r7, sums,
    in_sem, w_send, w_recv, f_send, f_recv, t_send, t_recv, e_send, e_recv,
    a_send, a_recv, x_send, x_recv, o_send, o_recv,
):
    ctx = lax.axis_index("ctx")
    ch = lax.axis_index("ch")
    z = lax.div(ctx, 4)
    q = lax.rem(ctx, 4)
    core = lax.rem(q, 2)
    y_hi = lax.div(q, 2)
    x = lax.div(ch, 2)
    y_lo = lax.rem(ch, 2)
    x0 = lax.rem(x, 2)
    x1 = lax.div(x, 2)
    near = lax.rem(x0 + x1, 2)
    far = x1
    near_ch = ch + 2 - 4 * x0
    far_ch = (3 - x) * 2 + y_lo
    sibling = ctx + 1 - 2 * core
    across = ctx + 2 - 4 * y_hi
    beyond = z * 4 + 3 - q
    up = lax.rem(ctx + 4, CTX)
    down = lax.rem(ctx + CTX - 4, CTX)

    loads = []
    for place, (src, dst) in enumerate(
        ((k_hbm, kb), (v_hbm, vb), (rate_hbm, rate), (res_hbm, res), (gain_hbm, gain), (q_hbm, qb))
    ):
        loads.append(pltpu.make_async_copy(src, dst, in_sem.at[place]))
        loads[-1].start()
    w_own = pltpu.make_async_copy(w_hbm, wbuf.at[q], in_sem.at[6])
    w_own.start()

    bar = pltpu.get_barrier_semaphore()

    def greet(c, h):
        pl.semaphore_signal(bar, inc=1, device_id=(c, h), device_id_type=MESH)

    for c in (sibling, across, beyond):
        greet(c, ch)

    def greet_z(k, carry):
        greet(lax.rem(ctx + 4 * k, CTX), ch)
        return carry

    lax.fori_loop(1, 8, greet_z, 0)
    def greet_ch(k, carry):
        greet(ctx, lax.rem(ch + k, 8))
        return carry

    lax.fori_loop(1, 8, greet_ch, 0)
    is_home = ch == z
    pl.semaphore_wait(bar, 17)

    for place in (0, 1, 2):
        loads[place].wait()
    chunk = lax.broadcasted_iota(jnp.int32, (POLES, CHUNKS, 128), 1)

    def lanes_of(g):
        return pl.ds(pl.multiple_of(g * 128, 128), 128)

    def half_of(c):
        return pl.ds(pl.multiple_of(c * 512, 512), 512)

    def tokens_at(p):
        return pl.ds(p, CHUNKS, stride=STEPS)

    def ending(g, carry):
        lanes = lanes_of(g)
        u[g] = kb[:, lanes].astype(F32) * vb[:, lanes].astype(F32)
        rows = rate[:, lanes]
        decay = spread(jnp.exp(-rows))
        state = jnp.zeros((POLES, CHUNKS, 128), F32)
        for p in range(STEPS):
            state = state * decay + u[g, tokens_at(p), :][None]
        for reach in (1, 2, 4):
            over = spread(jnp.exp(-rows * (STEPS * reach)))
            moved = pltpu.roll(state, reach, 1)
            state = state + jnp.where(chunk >= reach, over * moved, 0.0)
        before[g] = jnp.where(chunk >= 1, pltpu.roll(state, 1, 1), 0.0)
        fsend[lax.div(g, 4), :, lanes_of(lax.rem(g, 4))] = state[:, CHUNKS - 1, :]
        return carry

    lax.fori_loop(0, 8, ending, 0)

    f_copies = [
        pltpu.make_async_remote_copy(
            src_ref=fsend.at[half], dst_ref=fgroup.at[q], send_sem=f_send.at[place], recv_sem=f_recv.at[place],
            device_id=(target, ch), device_id_type=MESH,
        )
        for place, (half, target) in enumerate(((core, across), (1 - core, beyond), (1 - core, sibling)))
    ]
    for copy in f_copies:
        copy.start()

    def w_copy(src, slot, part, place, target):
        rows = pl.ds(part * 1024, 1024)
        return pltpu.make_async_remote_copy(
            src_ref=src.at[rows], dst_ref=wbuf.at[slot, rows],
            send_sem=w_send.at[place, part], recv_sem=w_recv.at[place, part],
            device_id=(target, ch), device_id_type=MESH,
        )

    w_across = [w_copy(w_hbm, q, part, 0, across) for part in range(1)]
    w_sibling = [w_copy(w_hbm, q, part, 1, sibling) for part in range(1)]
    for copy in (*w_across, *w_sibling):
        copy.start()
    fgroup[q] = fsend[core]

    for place in (3, 4, 5):
        loads[place].wait()

    def inside(g, carry):
        lanes = lanes_of(g)
        rows = rate[:, lanes]
        coef_rows = res[:, lanes] * jnp.sqrt(one_minus_exp(2.0 * rows))
        decay = spread(jnp.exp(-rows))
        coef = spread(coef_rows)
        lead[g] = coef * jnp.exp(-spread(rows) * (1.0 + STEPS * chunk.astype(F32)))
        direct = jnp.broadcast_to(gain[0:1, lanes], (CHUNKS, 128))
        qf[g] = qb[:, lanes].astype(F32)
        state = before[g]
        for p in range(STEPS):
            token = u[g, tokens_at(p), :]
            state = state * decay + token[None]
            y[g, tokens_at(p), :] = direct * token + jnp.sum(coef * state, axis=0)
        return carry

    lax.fori_loop(0, 8, inside, 0)

    for copy in f_copies:
        copy.wait_recv()
    half_rows = rate[:, half_of(core)]
    own_decay = jnp.exp(-half_rows * ROWS)
    group_decay = jnp.exp(-half_rows * (4 * ROWS))
    total = jnp.zeros((POLES, 512), F32)
    for i in range(4):
        dgroup[i] = total
        total = total * own_decay + fgroup[i]
    tsend[...] = total.astype(BF)

    def t_copy(dz):
        return pltpu.make_async_remote_copy(
            src_ref=tsend, dst_ref=trecv.at[z], send_sem=t_send.at[dz], recv_sem=t_recv.at[z],
            device_id=(lax.rem(ctx + 4 * dz, CTX), ch), device_id_type=MESH,
        )

    for dz in (4, 3, 5, 2, 6, 1, 7):
        @pl.when(z + dz < 8)
        def _():
            t_copy(dz).start()

    def earlier(i, so_far):
        pltpu.make_async_copy(trecv.at[i], trecv.at[i], t_recv.at[i]).wait()
        return so_far * group_decay + trecv[i].astype(F32)

    so_far = lax.fori_loop(0, z, earlier, jnp.zeros((POLES, 512), F32))

    def entry_of(place):
        return so_far * jnp.exp(-half_rows * (ROWS * place).astype(F32)) + dgroup[place]

    esend[...] = entry_of(q + 1 - 2 * core)
    e_copy = pltpu.make_async_remote_copy(
        src_ref=esend, dst_ref=entry.at[core], send_sem=e_send, recv_sem=e_recv,
        device_id=(sibling, ch), device_id_type=MESH,
    )
    e_copy.start()
    entry[core] = entry_of(q)

    def a_copy(r, way, c):
        src = 0 if r == 1 else 2 * (r - 1) - 1 + way
        dst = 7 if r == 4 else 2 * r - 1 + way
        place = ((r - 1) * 2 + way) * PARTS + c
        return pltpu.make_async_remote_copy(
            src_ref=abuf.at[src, pl.ds(c * 64, 64)], dst_ref=abuf.at[dst, pl.ds(c * 64, 64)],
            send_sem=a_send.at[place], recv_sem=a_recv.at[place],
            device_id=((up, down)[way], ch), device_id_type=MESH,
        )

    def finish(k, carry):
        g = lax.rem(4 * core + k, 8)
        lanes = lanes_of(g)
        decay = spread(jnp.exp(-rate[:, lanes]))
        rest = lead[g] * spread(entry[lax.div(g, 4), :, lanes_of(lax.rem(g, 4))])
        for p in range(STEPS):
            y[g, tokens_at(p), :] = qf[g, tokens_at(p), :] * (
                y[g, tokens_at(p), :] + jnp.sum(rest, axis=0)
            )
            rest = rest * decay
        abuf[0, :, lanes] = y[g].astype(BF)
        return carry

    a_copies = {}

    def a_go(r, way, c):
        a_copies[r, way, c] = a_copy(r, way, c)
        a_copies[r, way, c].start()

    def a_first(way, h):
        lanes = half_of(lax.rem(core + h, 2))
        place = 8 * PARTS + 2 * way + h
        return pltpu.make_async_remote_copy(
            src_ref=abuf.at[0, pl.ds(way * 64, 64), lanes], dst_ref=abuf.at[1 + way, pl.ds(way * 64, 64), lanes],
            send_sem=a_send.at[place], recv_sem=a_recv.at[place],
            device_id=((up, down)[way], ch), device_id_type=MESH,
        )

    firsts = [[a_first(way, h) for h in range(2)] for way in range(2)]
    lax.fori_loop(0, 4, finish, 0)
    for way in range(2):
        firsts[way][0].start()
    e_copy.wait_recv()
    lax.fori_loop(4, 8, finish, 0)
    for way in range(2):
        firsts[way][1].start()
    for way in range(2):
        a_go(1, way, 1 - way)

    def a_arrive(r, i):
        for way in range(2):
            c = (way + i) % 2
            for copy in firsts[way] if r == 1 and i == 0 else (a_copies[r, way, c],):
                copy.wait_recv()
            if r < 3 or (r == 3 and i == 0):
                a_go(r + 1, way, c)

    def product(left, side, store):
        def one(h, carry):
            total = jnp.dot(left(), wbuf[2 * side + h], preferred_element_type=F32)
            store(pl.ds(pl.multiple_of(h * 256, 256), 256), total.astype(BF))
            return carry

        lax.fori_loop(0, 2, one, 0)

    def rows_at(start, size):
        return pl.ds(pl.multiple_of(start, size), size)

    def first_bit(s):
        return near + s * (far - near)

    def second_bit(s):
        return far + s * (near - far)

    def first_ch(s):
        return near_ch + s * (far_ch - near_ch)

    def second_ch(s):
        return far_ch + s * (near_ch - far_ch)

    def runs_of(t):
        if t in (0, 7):
            return ((t, 0), (t, 64))
        r, second = (t + 1) // 2, (t + 1) % 2
        return ((2 * r - 1, 64 * second), (2 * r, 64 - 64 * second))

    def place_of(t, run):
        if t in (0, 7):
            return t // 7 * 4, 64 * run
        r, second = (t + 1) // 2, (t + 1) % 2
        return r * (2 * run - 1), (64 - 64 * run if second else 64 * run)

    def multiply(t, s):
        def left():
            return jnp.concatenate([abuf[j, row : row + 64] for j, row in runs_of(t)], axis=0)

        def store(columns, total):
            for run in range(2):
                part[t, run, s, :, columns] = total[run * 64 : (run + 1) * 64]

        product(left, s, store)

    def halves(t, s):
        multiply(t, s)
        pltpu.make_async_remote_copy(
            src_ref=part.at[t, 1 - first_bit(s), s], dst_ref=r1.at[t, s],
            send_sem=x_send.at[0], recv_sem=x_recv.at[t, s],
            device_id=(ctx, first_ch(s)), device_id_type=MESH,
        ).start()

    def quarters(t):
        for s in range(2):
            pltpu.make_async_copy(r1.at[t, s], r1.at[t, s], x_recv.at[t, s]).wait()
            p2[t, s] = (part[t, first_bit(s), s].astype(F32) + r1[t, s].astype(F32)).astype(BF)
            for place, (turn, y_turn) in enumerate(((1, 1), (1, 0), (0, 1))):
                bit = 1 - second_bit(s) if turn else second_bit(s)
                y_bit = 1 - y_lo if y_turn else y_lo
                target = second_ch(s) if turn else ch
                pltpu.make_async_remote_copy(
                    src_ref=p2.at[t, s, rows_at(bit * 32 + y_bit * 16, 16)], dst_ref=r2.at[t, s, place],
                    send_sem=x_send.at[1], recv_sem=x_recv.at[8 + t, s],
                    device_id=(ctx, target - y_lo + y_bit), device_id_type=MESH,
                ).start()

    def whole(t):
        for s in range(2):
            pltpu.make_async_copy(r2.at[t, s], r2.at[t, s], x_recv.at[8 + t, s]).wait()
            row = second_bit(s) * 32 + y_lo * 16
            total = p2[t, s, rows_at(row, 16), :].astype(F32)
            for place in range(3):
                total = total + r2[t, s, place].astype(F32)
            sums[t, s] = total.astype(BF)
            steps, start = place_of(t, first_bit(s))
            place_out(sums.at[t, s], steps, start + row, s, t == 0)

    def direct(t):
        for dy in (1, 0):
            owner_y = lax.rem(y_lo + dy, 2)
            multiply(t, owner_y)
            for place, (dx, turn) in enumerate(AROUND):
                if turn == dy:
                    owner_x = lax.rem(x + dx, 4)
                    pltpu.make_async_remote_copy(
                        src_ref=part.at[t, :, owner_y, rows_at(owner_x * 16, 16)], dst_ref=r7.at[t - STAGED, place],
                        send_sem=x_send.at[2], recv_sem=x_recv.at[8 + t, 0],
                        device_id=(ctx, owner_x * 2 + owner_y), device_id_type=MESH,
                    ).start()

    def direct_whole(t):
        came = r7.at[t - STAGED]
        pltpu.make_async_copy(came, came, x_recv.at[8 + t, 0]).wait()
        total = part[t, :, y_lo, rows_at(x * 16, 16), :].astype(F32)
        for place in range(len(AROUND)):
            total = total + r7[t - STAGED, place].astype(F32)
        sums[t] = total.astype(BF)
        for run in range(2):
            steps, start = place_of(t, run)
            place_out(sums.at[t, run], steps, start + x * 16, y_lo)

    def place_out(src, steps, row, s, own=False):
        dst = out_hbm.at[rows_at(row, 16), half_of(s)]
        block = lax.rem(z + steps + 8, 8)
        remote = pltpu.make_async_remote_copy(
            src_ref=src, dst_ref=dst, send_sem=o_send, recv_sem=o_recv,
            device_id=(block * 4 + q, z), device_id_type=MESH,
        )
        if own:
            @pl.when(is_home)
            def _():
                pltpu.make_async_copy(src, dst, o_recv).start()

            @pl.when(jnp.logical_not(is_home))
            def _():
                remote.start()
        else:
            remote.start()

    across_slot = lax.rem(q + 2, 4)
    w_onward = [w_copy(wbuf.at[across_slot], across_slot, part, 2, sibling) for part in range(1)]
    w_own.wait()
    for n in range(1):
        w_sibling[n].wait_recv()
    halves(0, y_hi)
    for n in range(1):
        w_across[n].wait_recv()
        w_onward[n].start()
    a_arrive(1, 0)
    for n in range(1):
        w_onward[n].wait_recv()
    halves(0, 1 - y_hi)
    halves(1, 0)
    halves(1, 1)
    a_arrive(1, 1)
    quarters(0)
    halves(2, 0)
    halves(2, 1)
    a_arrive(2, 0)
    quarters(1)
    halves(3, 0)
    halves(3, 1)
    a_arrive(2, 1)
    quarters(2)
    halves(4, 0)
    halves(4, 1)
    whole(0)
    a_arrive(3, 0)
    quarters(3)
    halves(5, 0)
    halves(5, 1)
    whole(1)
    a_arrive(3, 1)
    quarters(4)
    halves(6, 0)
    halves(6, 1)
    whole(2)
    quarters(5)
    a_arrive(4, 0)
    direct(7)
    quarters(6)
    whole(3)
    whole(4)
    whole(5)
    direct_whole(7)
    whole(6)

    for copy in (*f_copies, *w_across, *w_sibling, e_copy, *w_onward, *firsts[0], *firsts[1], *a_copies.values()):
        copy.wait_send()
    for dz in range(1, 8):
        @pl.when(z + dz < 8)
        def _():
            t_copy(dz).wait_send()

    pltpu.make_async_copy(r1, r1, x_send.at[0]).wait()
    pltpu.make_async_copy(r2, r2, x_send.at[1]).wait()
    pltpu.make_async_copy(r7, r7, x_send.at[2]).wait()
    later = sums.at[pl.ds(1, 7)]
    pltpu.make_async_copy(later, later, o_send).wait()

    @pl.when(jnp.logical_not(is_home))
    def _():
        pltpu.make_async_copy(sums.at[0], sums.at[0], o_send).wait()

    pltpu.make_async_copy(out_hbm, out_hbm, o_recv).wait()


def shards(query_proj, key_proj, value_proj, pole_rate, residue, direct_gain, out_weight):
    vmem = pltpu.VMEM
    dma = pltpu.SemaphoreType.DMA
    block = (ROWS, WIDTH)
    grouped = (8, ROWS, 128)
    tables = (8, POLES, CHUNKS, 128)
    return pl.pallas_call(
        kernel,
        out_shape=jax.ShapeDtypeStruct(block, BF),
        in_specs=[pl.BlockSpec(memory_space=pltpu.HBM)] * 7,
        out_specs=pl.BlockSpec(memory_space=pltpu.HBM),
        scratch_shapes=[
            vmem(block, BF), vmem(block, BF), vmem(block, BF),
            vmem((POLES, WIDTH), F32), vmem((POLES, WIDTH), F32), vmem((1, WIDTH), F32),
            vmem(grouped, F32), vmem(grouped, F32), vmem(grouped, F32),
            vmem(tables, F32), vmem(tables, F32),
            vmem((2, POLES, 512), F32), vmem((4, POLES, 512), F32), vmem((4, POLES, 512), F32),
            vmem((POLES, 512), BF), vmem((8, POLES, 512), BF),
            vmem((POLES, 512), F32), vmem((2, POLES, 512), F32),
            vmem((4, WIDTH, 256), BF), vmem((8, ROWS, WIDTH), BF), vmem((8, 2, 2, 64, 512), BF),
            vmem((STAGED, 2, 64, 512), BF), vmem((STAGED, 2, 64, 512), BF), vmem((STAGED, 2, 3, 16, 512), BF),
            vmem((8 - STAGED, len(AROUND), 2, 16, 512), BF), vmem((8, 2, 16, 512), BF),
            dma((7,)), dma((3, 2)), dma((3, 2)), dma((3,)), dma((3,)), dma((8,)), dma((8,)), dma, dma,
            dma((8 * PARTS + 4,)), dma((8 * PARTS + 4,)), dma((3,)), dma((16, 2)), dma, dma,
        ],
        compiler_params=pltpu.CompilerParams(
            collective_id=0, has_side_effects=True, vmem_limit_bytes=48 * 1024 * 1024
        ),
        cost_estimate=pl.CostEstimate(flops=2**31, bytes_accessed=2**21, transcendentals=2**18),
    )(
        *(
            pltpu.with_memory_space_constraint(a, pltpu.HBM)
            for a in (
                query_proj, key_proj, value_proj, pole_rate, residue,
                direct_gain.reshape(1, WIDTH), out_weight,
            )
        )
    )


def solution(mesh):
    return jax.shard_map(
        shards,
        mesh=mesh,
        in_specs=(
            P("ctx", "ch"),
            P("ctx", "ch"),
            P("ctx", "ch"),
            P(None, "ch"),
            P(None, "ch"),
            P("ch"),
            P("ch", "ctx"),
        ),
        out_specs=P("ctx", "ch"),
        check_vma=False,
    )
```
